128 devices in a mesh: chan: 32 (over x, z, y_hi), win: 4 (over y_lo, core).
Axes of the slice: x: 4, y: 4 (y_hi: 2, y_lo: 2; y = y_hi * 2 + y_lo), z: 4, core: 2. Of those that a mesh axis runs over, the one named last changes fastest.
Arguments:
- spectra: bfloat16 [2, 1024, 32, 768], P(None, 'chan', 'win'), may hold values from -6 to 6
- window_flags: int32 [32], P('win'), may hold values 0 or 1
- source_block: int32 [4], replicated, may hold values from 0 to 31
- offset_limit: int32 [4], replicated, may hold values from 32 to 1023
Outputs:
- correlations: bfloat16 [4, 32, 1024, 1536], P(None, 'win', 'chan')
The draws below stay inside these ranges and needn't reach their ends.
All inputs are finite; a program needn't handle non-finite values. No bound on the sum of `window_flags` on one device may be relied on, other than what follows from the above.
Results may differ from the reference program's by a relative error of at most 0.0055.
Values may be sent and summed in bfloat16 or wider, within the bound.
A program may use at most 192 MiB of HBM per device.

```python
import math
import jax
import jax.numpy as jnp
from jax import lax

CH_DEV = 32
F = 768
ROUNDS = 4
C = 1024
WINDOWS = 32
N_CHAN = 32


def set_ends(result, own_key, least, largest):
    dims = result.shape
    spot = [jax.random.randint(jax.random.fold_in(own_key, axis), (), 0, dims[axis]) for axis in range(len(dims))]
    result = result.at[tuple(spot)].set(least)
    longest = dims.index(max(dims))
    spot[longest] = (spot[longest] + 1) % dims[longest]
    return result.at[tuple(spot)].set(largest)


def shard_levels(stream_key, extent, split, smallest, top_value):
    def one(axis_at, blocks):
        heights = jax.random.uniform(jax.random.fold_in(jax.random.fold_in(stream_key, 6), axis_at), (blocks,), jnp.float32, smallest / len(split), top_value / len(split))
        return jnp.repeat(jnp.exp(heights), extent[axis_at] // blocks).reshape((-1,) + (1,) * (len(extent) - axis_at - 1))

    loudness = one(*split[0])
    for cut in split[1:]:
        loudness = loudness * one(*cut)
    return loudness


def scatter_about(stream_key, extent, scale, limit, shards=(), kind=jnp.bfloat16):
    factor_of = shard_levels(stream_key, extent, shards, -0.22, 0.18) if shards else 1.0
    values = jax.random.normal(stream_key, extent, jnp.float32) * scale * factor_of
    return jnp.minimum(jnp.maximum(values, -limit), limit).astype(kind)


def setup_inputs(seed: int = 0) -> dict:
    key_list = jax.random.split(jax.random.key(seed), 5)
    return {
        "spectra": scatter_about(key_list[0], (2, C, WINDOWS, F), 1.0, 6.0, ((1, 32), (2, 4))),
        "window_flags": set_ends((jax.random.randint(key_list[1], (WINDOWS,), 0, 4) < 3).astype(jnp.int32), jax.random.fold_in(key_list[1], 1), 0, 1),
        "source_block": set_ends(jax.random.randint(key_list[2], (ROUNDS,), 0, N_CHAN), jax.random.fold_in(key_list[2], 1), 0, N_CHAN - 1).astype(jnp.int32),
        "offset_limit": set_ends(jax.random.randint(key_list[3], (ROUNDS,), CH_DEV, C), jax.random.fold_in(key_list[3], 1), CH_DEV, C - 1).astype(jnp.int32),
    }


def whiten(spectra):
    real = spectra[0].astype(jnp.float32)
    imag = spectra[1].astype(jnp.float32)
    power = real * real + imag * imag
    level = lax.optimization_barrier(jnp.mean(power, axis=-1, keepdims=True))
    factor = lax.rsqrt(power + 0.25 * level + 1e-06)
    return jnp.stack([real * factor, imag * factor]).astype(jnp.bfloat16)

def lag_table(bins, windows):
    freq = jnp.arange(bins, dtype=jnp.int32)
    shifts = jnp.arange(2 * bins, dtype=jnp.int32) - bins
    phase = jnp.mod(freq[:, None] * shifts[None, :], 2 * bins).astype(jnp.float32)
    theta = phase * (math.pi / bins)
    weight = jnp.where(freq == 0, 1.0, 2.0).astype(jnp.float32) / math.sqrt(bins * windows)
    return jnp.concatenate([weight[:, None] * jnp.cos(theta), -weight[:, None] * jnp.sin(theta)], axis=0)

def reference(spectra, window_flags, source_block, offset_limit):
    white = whiten(spectra)
    flags = window_flags.astype(jnp.float32)
    recv_real = white[0].astype(jnp.float32) * flags[None, :, None]
    recv_imag = white[1].astype(jnp.float32) * flags[None, :, None]
    table = lag_table(F, WINDOWS)
    receivers = jnp.arange(C, dtype=jnp.int32)
    results = []
    for step in range(ROUNDS):
        start = (source_block[step] * CH_DEV).astype(jnp.int32)
        source = lax.dynamic_slice_in_dim(white, start, CH_DEV, 1).astype(jnp.float32)
        real = jnp.einsum('swf,cwf->scf', source[0], recv_real) + jnp.einsum('swf,cwf->scf', source[1], recv_imag)
        imag = jnp.einsum('swf,cwf->scf', source[0], recv_imag) - jnp.einsum('swf,cwf->scf', source[1], recv_real)
        senders = start + jnp.arange(CH_DEV, dtype=jnp.int32)
        gap = jnp.abs(receivers[None, :] - senders[:, None])
        keep = ((gap >= 1) & (gap <= offset_limit[step])).astype(jnp.float32)
        stack = jnp.concatenate([real * keep[..., None], imag * keep[..., None]], axis=-1)
        corr = jnp.einsum('scf,fl->scl', stack, table, precision=lax.Precision.HIGHEST)
        results.append(corr.astype(jnp.bfloat16))
    return jnp.stack(results)
```

```python
import math

import jax
import jax.numpy as jnp
import numpy as np
from jax import lax
from jax.experimental import pallas as pl
from jax.experimental.pallas import tpu as pltpu
from jax.sharding import PartitionSpec as P

MESH = pl.DeviceIdType.MESH
F = 768
HALF = 384
R = 4
SCALE = 1.0 / math.sqrt(24576.0)


def constants():
    rows = np.zeros((256, 256), np.float32)
    for wp in range(4):
        for p in range(4):
            for w2 in range(2):
                for c in range(8):
                    rows[((wp * 4 + p) * 2 + w2) * 8 + c, (p * 8 + c) * 8 + wp * 2 + w2] = 1.0
    cols = np.zeros((256, 256), np.float32)
    for i in range(128):
        cols[2 * i, i] = 1.0
        cols[2 * i + 1, 128 + i] = 1.0
    k = (256 * np.arange(3)[:, None] + 2 * np.arange(128)[None, :]).reshape(-1)
    lag = np.arange(768) - 768
    table = np.zeros((2, 768, 768), np.float32)
    for h in range(2):
        kk = k + h
        m = (kk[:, None] * lag[None, :]) % 1536
        g = np.where(kk == 0, 1.0, 2.0)[:, None]
        table[h, :HALF] = g * np.cos(np.pi * m / 768.0)
        table[h, HALF:] = -g * np.sin(np.pi * m / 768.0)
    return rows, cols, table


def coords():
    c, w = lax.axis_index("chan"), lax.axis_index("win")
    return c // 8, (c // 2) % 4, c % 2, w


def dev(x, z, yh, j):
    return (x * 8 + z * 2 + yh, j)


def whiten_into(spec_ref, flag_ref, rows_ref, cols_ref, out):
    for wp in range(4):
        part = []
        for reim in range(2):
            moved = jnp.dot(rows_ref[pl.ds(wp * 64, 64), :], spec_ref[reim], preferred_element_type=jnp.float32)
            moved = moved.astype(jnp.bfloat16)
            cut = [
                jnp.dot(moved[:, 256 * b:256 * b + 256], cols_ref[...], preferred_element_type=jnp.float32)
                for b in range(3)
            ]
            even = jnp.concatenate([c[:, :128] for c in cut], axis=1)
            odd = jnp.concatenate([c[:, 128:] for c in cut], axis=1)
            part.append((even, odd))
        (re0, re1), (im0, im1) = part
        p0 = re0 * re0 + im0 * im0
        p1 = re1 * re1 + im1 * im1
        level = (jnp.sum(p0, axis=1, keepdims=True) + jnp.sum(p1, axis=1, keepdims=True)) * (1.0 / F)
        base = 0.25 * level + 1e-06
        row = lax.broadcasted_iota(jnp.int32, (64, 1), 0)
        f0 = flag_ref[2 * wp].astype(jnp.float32)
        f1 = flag_ref[2 * wp + 1].astype(jnp.float32)
        flag = jnp.where((row // 8) % 2 == 0, f0, f1)
        q0 = lax.rsqrt(p0 + base) * flag
        q1 = lax.rsqrt(p1 + base) * flag
        for reim, h, v in ((0, 0, re0 * q0), (0, 1, re1 * q1), (1, 0, im0 * q0), (1, 1, im1 * q1)):
            out[reim * 8 + wp * 2 + h] = v.astype(jnp.bfloat16).reshape(4, 16, HALF)


def comm_kernel(block_ref, flag_ref, spec_ref, rows_ref, cols_ref, recv_out, src_out,
                recv, cand, pick, diag, src,
                a_s, a_r, d_s, d_r, p_s, p_r, g_s, g_r, f_s, f_r, o_s, t_s, t_r, u_s, u_r):
    x, z, yh, j = coords()
    slot = x * 4 + z
    bar = pltpu.get_barrier_semaphore()
    plane = []
    for t in range(1, 16):
        to = (slot + t) % 16
        plane.append((to, dev(to // 4, to % 4, yh, j)))
    column = []
    for t in range(1, 8):
        column.append((t, (j + t) % 4, dev(x, z, (yh + t // 4) % 2, (j + t) % 4)))
    for _, d in plane:
        pl.semaphore_signal(bar, inc=1, device_id=d, device_id_type=MESH)
    for _, _, d in column:
        pl.semaphore_signal(bar, inc=1, device_id=d, device_id_type=MESH)

    whiten_into(spec_ref, flag_ref, rows_ref, cols_ref, recv.at[j])
    pl.semaphore_wait(bar, 22)
    sends = []

    def send(s, d, ss, rs, to):
        c = pltpu.make_async_remote_copy(
            src_ref=s, dst_ref=d, send_sem=ss, recv_sem=rs, device_id=to, device_id_type=MESH)
        c.start()
        sends.append(c)
        return c

    mate = dev(x, z, yh, j + 1 - 2 * (j % 2))
    across = (j + 2) % 4
    other = dev(x, z, yh, across)
    swap = [send(recv.at[j, to], cand.at[slot], a_s.at[t], a_r.at[t], d) for t, (to, d) in enumerate(plane)]
    over = [
        send(recv.at[j, pl.ds(4 * q, 4)], recv.at[j, pl.ds(4 * q, 4)], g_s.at[q], g_r.at[q], other)
        for q in range(4)
    ]
    to_mate = send(recv.at[j], recv.at[j], p_s.at[0], p_r.at[0], mate)
    cand[slot] = recv[j, slot]

    relayed = []

    def relay(q):
        over[q].wait_recv()
        relayed.append(send(recv.at[across, pl.ds(4 * q, 4)], recv.at[across, pl.ds(4 * q, 4)], f_s.at[q], f_r.at[q], mate))

    for c in swap:
        c.wait_recv()
    for r in range(R):
        pick[:, r] = cand[block_ref[r] // 2]
    meet = [send(pick.at[p], diag.at[yh, j], d_s.at[t], d_r.at[t], d) for t, p, d in column]
    diag[yh, j] = pick[j]
    relay(0)
    for c in meet:
        c.wait_recv()
    for r in range(R):
        got = diag[block_ref[r] % 2, :, r]
        src[0, r, x, z] = got[0:2]
        src[1, r, x, z] = got[2:4]
    first = []
    for d in range(1, 4):
        z2, x2 = (z + d) % 4, (x + d) % 4
        first.append(send(src.at[0, :, x, z], src.at[0, :, x, z], t_s.at[0, d], t_r.at[0, d], dev(x, z2, yh, j)))
        first.append(send(src.at[1, :, x, z], src.at[1, :, x, z], t_s.at[1, d], t_r.at[1, d], dev(x2, z, yh, j)))
    relay(1)
    for c in first:
        c.wait_recv()
    second = []
    for r in range(R):
        for d in range(1, 4):
            z2, x2 = (z + d) % 4, (x + d) % 4
            second.append(send(src.at[0, r, x], src.at[0, r, x], u_s.at[0, r, d], u_r.at[0, r, d], dev(x2, z, yh, j)))
            second.append(send(src.at[1, r, :, z], src.at[1, r, :, z], u_s.at[1, r, d], u_r.at[1, r, d], dev(x, z2, yh, j)))
    relay(2)
    relay(3)
    to_mate.wait_recv()
    for c in relayed:
        c.wait_recv()
    out1 = pltpu.make_async_copy(recv, recv_out, o_s.at[0])
    out1.start()
    for c in second:
        c.wait_recv()
    out2 = pltpu.make_async_copy(src, src_out, o_s.at[1])
    out2.start()
    out1.wait()
    out2.wait()
    for c in sends:
        c.wait_send()


def comm(block, flags, spec, rows, cols):
    bf = jnp.bfloat16
    dma = pltpu.SemaphoreType.DMA
    vm = pl.BlockSpec(memory_space=pltpu.VMEM)
    sm = pl.BlockSpec(memory_space=pltpu.SMEM)
    return pl.pallas_call(
        comm_kernel,
        out_shape=(
            jax.ShapeDtypeStruct((4, 16, 4, 16, HALF), bf),
            jax.ShapeDtypeStruct((2, R, 4, 4, 2, 16, HALF), bf),
        ),
        in_specs=[sm, sm, vm, vm, vm],
        out_specs=[pl.BlockSpec(memory_space=pl.ANY)] * 2,
        scratch_shapes=[
            pltpu.VMEM((4, 16, 4, 16, HALF), bf),
            pltpu.VMEM((16, 4, 16, HALF), bf),
            pltpu.VMEM((4, R, 16, HALF), bf),
            pltpu.VMEM((2, 4, R, 16, HALF), bf),
            pltpu.VMEM((2, R, 4, 4, 2, 16, HALF), bf),
            dma((16,)), dma((16,)), dma((8,)), dma((8,)), dma((1,)), dma((1,)),
            dma((4,)), dma((4,)), dma((4,)), dma((4,)), dma((2,)),
            dma((2, 4)), dma((2, 4)), dma((2, R, 4)), dma((2, R, 4)),
        ],
        compiler_params=pltpu.CompilerParams(
            collective_id=1, has_side_effects=True, vmem_limit_bytes=50 * 2**20),
        name="comm",
    )(block, flags, spec, rows, cols)


def corr_kernel(block_ref, limit_ref, recv_ref, src_ref, table_ref, out_ref,
                xr, xi, yr, yi, yd, stack):
    chan, member = lax.axis_index("chan"), lax.axis_index("win")
    r = pl.program_id(0)

    @pl.when(r == 0)
    def _():
        @pl.loop(0, 16)
        def _(n):
            a, wp = n // 4, n % 4
            for h in range(2):
                for reim, to in ((0, xr), (1, xi)):
                    for p in range(4):
                        v = recv_ref[a, reim * 8 + wp * 2 + h, p].astype(jnp.float32)
                        for b in range(3):
                            for w2 in range(2):
                                to[h * 3 + b, n * 2 + w2, p] = v[8 * w2:8 * w2 + 8, 128 * b:128 * b + 128]

    @pl.loop(0, 16)
    def _(n):
        a, wp = n // 4, n % 4
        for h in range(2):
            lo, hi = wp * 2 + h, 8 + wp * 2 + h
            vr = src_ref[a // 2, 0, lo // 4, lo % 4, a % 2].astype(jnp.float32)
            vi = src_ref[a // 2, 0, hi // 4, hi % 4, a % 2].astype(jnp.float32)
            for b in range(3):
                for w2 in range(2):
                    cr = vr[8 * w2:8 * w2 + 8, 128 * b:128 * b + 128]
                    ci = vi[8 * w2:8 * w2 + 8, 128 * b:128 * b + 128]
                    yr[h * 3 + b, n * 2 + w2] = cr
                    yi[h * 3 + b, n * 2 + w2] = ci
                    yd[h * 3 + b, n * 2 + w2] = cr - ci

    root, limit = block_ref[r], limit_ref[r]
    c8 = lax.broadcasted_iota(jnp.int32, (8, 1), 0)
    SB = 2
    for h in range(2):
        @pl.loop(0, 3 * (8 // SB))
        def _(n):
            b, s0 = n // (8 // SB), (n % (8 // SB)) * SB
            kt = h * 3 + b

            def step(w, acc):
                acc = list(acc)
                for u in range(4):
                    ww = w * 4 + u
                    ar = [xr[kt, ww, p] for p in range(4)]
                    ai = [xi[kt, ww, p] for p in range(4)]
                    asum = [ar[p] + ai[p] for p in range(4)]
                    for s in range(SB):
                        br = jnp.broadcast_to(yr[kt, ww, pl.ds(s0 + s, 1)], (8, 128))
                        bi = jnp.broadcast_to(yi[kt, ww, pl.ds(s0 + s, 1)], (8, 128))
                        bd = jnp.broadcast_to(yd[kt, ww, pl.ds(s0 + s, 1)], (8, 128))
                        for p in range(4):
                            i = (s * 4 + p) * 3
                            acc[i] = acc[i] + ar[p] * br
                            acc[i + 1] = acc[i + 1] + ai[p] * bi
                            acc[i + 2] = acc[i + 2] + asum[p] * bd
                return tuple(acc)

            zero = jnp.zeros((8, 128), jnp.float32)
            acc = lax.fori_loop(0, 8, step, (zero,) * (SB * 12))
            for s in range(SB):
                sender = root * 32 + member * 8 + s0 + s
                re, im = [], []
                for p in range(4):
                    p1, p2, p3 = acc[(s * 4 + p) * 3:(s * 4 + p) * 3 + 3]
                    gap = jnp.abs(chan * 32 + p * 8 + c8 - sender)
                    keep = jnp.where((gap >= 1) & (gap <= limit), SCALE, 0.0)
                    re.append((p1 + p2) * keep)
                    im.append((p3 - p1 + p2) * keep)
                row = pl.multiple_of((s0 + s) * 32, 32)
                stack[h, b, pl.ds(row, 32), :] = jnp.concatenate(re, axis=0).astype(jnp.bfloat16)
                stack[h, 3 + b, pl.ds(row, 32), :] = jnp.concatenate(im, axis=0).astype(jnp.bfloat16)

    lhs = [jnp.concatenate([stack[h, b] for b in range(6)], axis=1) for h in range(2)]
    for n in range(3):
        cut = pl.ds(256 * n, 256)
        e = jnp.dot(lhs[0], table_ref[0, :, cut], preferred_element_type=jnp.float32)
        o = jnp.dot(lhs[1], table_ref[1, :, cut], preferred_element_type=jnp.float32)
        out_ref[0, :, pl.ds(256 * n, 256)] = (e + o).astype(jnp.bfloat16)
        out_ref[0, :, pl.ds(768 + 256 * n, 256)] = (e - o).astype(jnp.bfloat16)


def correlate(block, limit, recv, src, table):
    f32 = jnp.float32
    sm = pl.BlockSpec(memory_space=pltpu.SMEM)
    return pl.pallas_call(
        corr_kernel,
        grid=(R,),
        out_shape=jax.ShapeDtypeStruct((R, 256, 2 * F), jnp.bfloat16),
        in_specs=[
            sm, sm,
            pl.BlockSpec((4, 16, 4, 16, HALF), lambda r: (0, 0, 0, 0, 0)),
            pl.BlockSpec((2, 1, 4, 4, 2, 16, HALF), lambda r: (0, r, 0, 0, 0, 0, 0)),
            pl.BlockSpec((2, F, F), lambda r: (0, 0, 0)),
        ],
        out_specs=pl.BlockSpec((1, 256, 2 * F), lambda r: (r, 0, 0)),
        scratch_shapes=[
            pltpu.VMEM((6, 32, 4, 8, 128), f32), pltpu.VMEM((6, 32, 4, 8, 128), f32),
            pltpu.VMEM((6, 32, 8, 128), f32), pltpu.VMEM((6, 32, 8, 128), f32), pltpu.VMEM((6, 32, 8, 128), f32),
            pltpu.VMEM((2, 6, 256, 128), jnp.bfloat16),
        ],
        compiler_params=pltpu.CompilerParams(vmem_limit_bytes=50 * 2**20),
        name="correlate",
    )(block, limit, recv, src, table)


def shards(spectra, window_flags, source_block, offset_limit):
    rows, cols, table = constants()
    bf = jnp.bfloat16
    spec = spectra.reshape(2, 256, F)
    recv, src = comm(source_block, window_flags, spec, jnp.asarray(rows, bf), jnp.asarray(cols, bf))
    out = correlate(source_block, offset_limit, recv, src, jnp.asarray(table, bf))
    return out.reshape(R, 8, 32, 2 * F)


def solution(mesh):
    in_specs = (P(None, "chan", "win", None), P("win"), P(), P())
    out_specs = P(None, "win", "chan", None)
    return jax.shard_map(shards, mesh=mesh, in_specs=in_specs, out_specs=out_specs, check_vma=False)
```

```python
import math

import jax
import jax.numpy as jnp
import numpy as np
from jax import lax
from jax.experimental import pallas as pl
from jax.experimental.pallas import tpu as pltpu
from jax.sharding import PartitionSpec as P

MESH = pl.DeviceIdType.MESH
F = 768
HALF = 384
R = 4
SCALE = 1.0 / math.sqrt(24576.0)


def constants():
    rows = np.zeros((256, 256), np.float32)
    for wp in range(4):
        for p in range(4):
            for w2 in range(2):
                for c in range(8):
                    rows[((wp * 4 + p) * 2 + w2) * 8 + c, (p * 8 + c) * 8 + wp * 2 + w2] = 1.0
    cols = np.zeros((256, 256), np.float32)
    for i in range(128):
        cols[2 * i, i] = 1.0
        cols[2 * i + 1, 128 + i] = 1.0
    k = (256 * np.arange(3)[:, None] + 2 * np.arange(128)[None, :]).reshape(-1)
    lag = np.arange(768) - 768
    table = np.zeros((2, 768, 768), np.float32)
    for h in range(2):
        kk = k + h
        m = (kk[:, None] * lag[None, :]) % 1536
        g = np.where(kk == 0, 1.0, 2.0)[:, None]
        table[h, :HALF] = g * np.cos(np.pi * m / 768.0)
        table[h, HALF:] = -g * np.sin(np.pi * m / 768.0)
    return rows, cols, table


def coords():
    c, w = lax.axis_index("chan"), lax.axis_index("win")
    return c // 8, (c // 2) % 4, c % 2, w


def dev(x, z, yh, j):
    return (x * 8 + z * 2 + yh, j)


def whiten_into(spec_ref, flag_ref, rows_ref, cols_ref, out):
    for wp in range(4):
        part = []
        for reim in range(2):
            moved = jnp.dot(rows_ref[pl.ds(wp * 64, 64), :], spec_ref[reim], preferred_element_type=jnp.float32)
            moved = moved.astype(jnp.bfloat16)
            cut = [
                jnp.dot(moved[:, 256 * b:256 * b + 256], cols_ref[...], preferred_element_type=jnp.float32)
                for b in range(3)
            ]
            even = jnp.concatenate([c[:, :128] for c in cut], axis=1)
            odd = jnp.concatenate([c[:, 128:] for c in cut], axis=1)
            part.append((even, odd))
        (re0, re1), (im0, im1) = part
        p0 = re0 * re0 + im0 * im0
        p1 = re1 * re1 + im1 * im1
        level = (jnp.sum(p0, axis=1, keepdims=True) + jnp.sum(p1, axis=1, keepdims=True)) * (1.0 / F)
        base = 0.25 * level + 1e-06
        row = lax.broadcasted_iota(jnp.int32, (64, 1), 0)
        f0 = flag_ref[2 * wp].astype(jnp.float32)
        f1 = flag_ref[2 * wp + 1].astype(jnp.float32)
        flag = jnp.where((row // 8) % 2 == 0, f0, f1)
        q0 = lax.rsqrt(p0 + base) * flag
        q1 = lax.rsqrt(p1 + base) * flag
        for reim, h, v in ((0, 0, re0 * q0), (0, 1, re1 * q1), (1, 0, im0 * q0), (1, 1, im1 * q1)):
            out[reim * 8 + wp * 2 + h] = v.astype(jnp.bfloat16).reshape(4, 16, HALF)


def spread_receivers(recv, xr, xi):
    @pl.loop(0, 16)
    def _(n):
        a, wp = n // 4, n % 4
        for h in range(2):
            for reim, to in ((0, xr), (1, xi)):
                for p in range(4):
                    v = recv[a, reim * 8 + wp * 2 + h, p].astype(jnp.float32)
                    for b in range(3):
                        for w2 in range(2):
                            to[h * 3 + b, n * 2 + w2, p] = v[8 * w2:8 * w2 + 8, 128 * b:128 * b + 128]


def spread_sources(src, r, yr, yi, yd):
    @pl.loop(0, 16)
    def _(n):
        a, wp = n // 4, n % 4
        for h in range(2):
            lo, hi = wp * 2 + h, 8 + wp * 2 + h
            vr = src[a // 2, r, lo // 4, lo % 4, a % 2].astype(jnp.float32)
            vi = src[a // 2, r, hi // 4, hi % 4, a % 2].astype(jnp.float32)
            for b in range(3):
                for w2 in range(2):
                    cr = vr[8 * w2:8 * w2 + 8, 128 * b:128 * b + 128]
                    ci = vi[8 * w2:8 * w2 + 8, 128 * b:128 * b + 128]
                    yr[h * 3 + b, n * 2 + w2] = cr
                    yi[h * 3 + b, n * 2 + w2] = ci
                    yd[h * 3 + b, n * 2 + w2] = cr - ci


SB = 4
UNROLL = 8


def cross_round(xr, xi, yr, yi, yd, stack, root, limit, chan, member):
    c8 = lax.broadcasted_iota(jnp.int32, (8, 1), 0)

    @pl.loop(0, 6)
    def _(kt):
        for s0 in range(0, 8, SB):
            def step(w, acc):
                acc = list(acc)
                for u in range(UNROLL):
                    ww = w * UNROLL + u
                    ar = [xr[kt, ww, p] for p in range(4)]
                    ai = [xi[kt, ww, p] for p in range(4)]
                    asum = [ar[p] + ai[p] for p in range(4)]
                    for s in range(SB):
                        br = jnp.broadcast_to(yr[kt, ww, pl.ds(s0 + s, 1)], (8, 128))
                        bi = jnp.broadcast_to(yi[kt, ww, pl.ds(s0 + s, 1)], (8, 128))
                        bd = jnp.broadcast_to(yd[kt, ww, pl.ds(s0 + s, 1)], (8, 128))
                        for p in range(4):
                            i = (s * 4 + p) * 3
                            acc[i] = acc[i] + ar[p] * br
                            acc[i + 1] = acc[i + 1] + ai[p] * bi
                            acc[i + 2] = acc[i + 2] + asum[p] * bd
                return tuple(acc)

            zero = jnp.zeros((8, 128), jnp.float32)
            acc = lax.fori_loop(0, 32 // UNROLL, step, (zero,) * (SB * 12))
            for s in range(SB):
                sender = root * 32 + member * 8 + s0 + s
                re, im = [], []
                for p in range(4):
                    p1, p2, p3 = acc[(s * 4 + p) * 3:(s * 4 + p) * 3 + 3]
                    gap = jnp.abs(chan * 32 + p * 8 + c8 - sender)
                    keep = jnp.where((gap >= 1) & (gap <= limit), SCALE, 0.0)
                    re.append((p1 + p2) * keep)
                    im.append((p3 - p1 + p2) * keep)
                row = (s0 + s) * 32
                stack[kt // 3, kt % 3, pl.ds(row, 32), :] = jnp.concatenate(re, axis=0).astype(jnp.bfloat16)
                stack[kt // 3, 3 + kt % 3, pl.ds(row, 32), :] = jnp.concatenate(im, axis=0).astype(jnp.bfloat16)


def lag_round(stack, table, out, r):
    lhs = [jnp.concatenate([stack[h, b] for b in range(6)], axis=1) for h in range(2)]
    for n in range(3):
        cut = pl.ds(256 * n, 256)
        e = jnp.dot(lhs[0], table[0, :, cut], preferred_element_type=jnp.float32)
        o = jnp.dot(lhs[1], table[1, :, cut], preferred_element_type=jnp.float32)
        out[r, :, pl.ds(256 * n, 256)] = (e + o).astype(jnp.bfloat16)
        out[r, :, pl.ds(768 + 256 * n, 256)] = (e - o).astype(jnp.bfloat16)


def kernel(block_ref, limit_ref, flag_ref, spec_hbm, rows_hbm, cols_hbm, table_hbm, out_hbm,
           spec, rows, cols, table, recv, cand, pick, diag, src, xr, xi, yr, yi, yd, stack, out,
           a_s, a_r, d_s, d_r, p_s, p_r, g_s, g_r, f_s, f_r, i_s, o_s, t_s, t_r, u_s, u_r):
    x, z, yh, j = coords()
    slot = x * 4 + z
    bar = pltpu.get_barrier_semaphore()
    plane = []
    for t in range(1, 16):
        to = (slot + t) % 16
        plane.append((to, dev(to // 4, to % 4, yh, j)))
    column = []
    for t in range(1, 8):
        column.append((t, (j + t) % 4, dev(x, z, (yh + t // 4) % 2, (j + t) % 4)))
    loads = [
        pltpu.make_async_copy(s, d, i_s.at[n])
        for n, (s, d) in enumerate(((spec_hbm, spec), (rows_hbm, rows), (cols_hbm, cols), (table_hbm, table)))
    ]
    for c in loads:
        c.start()
    for _, d in plane:
        pl.semaphore_signal(bar, inc=1, device_id=d, device_id_type=MESH)
    for _, _, d in column:
        pl.semaphore_signal(bar, inc=1, device_id=d, device_id_type=MESH)

    for c in loads[:3]:
        c.wait()
    whiten_into(spec, flag_ref, rows, cols, recv.at[j])
    pl.semaphore_wait(bar, 22)
    sends = []

    def remote(s, d, ss, rs, to):
        return pltpu.make_async_remote_copy(
            src_ref=s, dst_ref=d, send_sem=ss, recv_sem=rs, device_id=to, device_id_type=MESH)

    def send(*args):
        c = remote(*args)
        c.start()
        sends.append(c)
        return c

    mate = dev(x, z, yh, j + 1 - 2 * (j % 2))
    across = (j + 2) % 4
    other = dev(x, z, yh, across)
    swap = [send(recv.at[j, to], cand.at[slot], a_s.at[t], a_r.at[t], d) for t, (to, d) in enumerate(plane)]
    over = [
        send(recv.at[j, pl.ds(4 * q, 4)], recv.at[j, pl.ds(4 * q, 4)], g_s.at[q], g_r.at[q], other)
        for q in range(4)
    ]
    to_mate = send(recv.at[j], recv.at[j], p_s.at[0], p_r.at[0], mate)
    cand[slot] = recv[j, slot]

    relayed = []

    def relay(q):
        over[q].wait_recv()
        relayed.append(send(recv.at[across, pl.ds(4 * q, 4)], recv.at[across, pl.ds(4 * q, 4)], f_s.at[q], f_r.at[q], mate))

    for c in swap:
        c.wait_recv()
    for r in range(R):
        pick[:, r] = cand[block_ref[r] // 2]
    meet = [send(pick.at[p], diag.at[yh, j], d_s.at[t], d_r.at[t], d) for t, p, d in column]
    diag[yh, j] = pick[j]
    relay(0)
    for c in meet:
        c.wait_recv()
    first = []
    for r in range(R):
        got = diag[block_ref[r] % 2, :, r]
        src[0, r, x, z] = got[0:2]
        src[1, r, x, z] = got[2:4]
        one = []
        for d in range(1, 4):
            z2, x2 = (z + d) % 4, (x + d) % 4
            one.append(send(src.at[0, r, x, z], src.at[0, r, x, z], t_s.at[0, r, d], t_r.at[0, r, d], dev(x, z2, yh, j)))
            one.append(send(src.at[1, r, x, z], src.at[1, r, x, z], t_s.at[1, r, d], t_r.at[1, r, d], dev(x2, z, yh, j)))
        first.append(one)
    relay(1)

    def spread(r, d):
        z2, x2 = (z + d) % 4, (x + d) % 4
        return (
            remote(src.at[0, r, x], src.at[0, r, x], u_s.at[0, r, d], u_r.at[0, r, d], dev(x2, z, yh, j)),
            remote(src.at[1, r, :, z], src.at[1, r, :, z], u_s.at[1, r, d], u_r.at[1, r, d], dev(x, z2, yh, j)),
        )

    for r in range(R):
        for c in first[r]:
            c.wait_recv()
        for d in range(1, 4):
            for c in spread(r, d):
                c.start()
    relay(2)
    relay(3)
    to_mate.wait_recv()
    for c in relayed:
        c.wait_recv()
    spread_receivers(recv, xr, xi)
    loads[3].wait()
    chan = x * 8 + z * 2 + yh

    @pl.loop(0, R)
    def _(r):
        for d in range(1, 4):
            for c in spread(r, d):
                c.wait_recv()
        spread_sources(src, r, yr, yi, yd)
        cross_round(xr, xi, yr, yi, yd, stack, block_ref[r], limit_ref[r], chan, j)
        lag_round(stack, table, out, r)
        pltpu.make_async_copy(out.at[r], out_hbm.at[r], o_s.at[r]).start()

    for r in range(R):
        pltpu.make_async_copy(out.at[r], out_hbm.at[r], o_s.at[r]).wait()
        for d in range(1, 4):
            for c in spread(r, d):
                c.wait_send()
    for c in sends:
        c.wait_send()


def fused(block, limit, flags, spec, rows, cols, table):
    bf, f32 = jnp.bfloat16, jnp.float32
    dma = pltpu.SemaphoreType.DMA
    hbm = pl.BlockSpec(memory_space=pl.ANY)
    sm = pl.BlockSpec(memory_space=pltpu.SMEM)
    vm = pltpu.VMEM
    return pl.pallas_call(
        kernel,
        out_shape=jax.ShapeDtypeStruct((R, 256, 2 * F), bf),
        in_specs=[sm, sm, sm, hbm, hbm, hbm, hbm],
        out_specs=hbm,
        scratch_shapes=[
            vm((2, 256, F), bf), vm((256, 256), bf), vm((256, 256), bf), vm((2, F, F), bf),
            vm((4, 16, 4, 16, HALF), bf),
            vm((16, 4, 16, HALF), bf),
            vm((4, R, 16, HALF), bf),
            vm((2, 4, R, 16, HALF), bf),
            vm((2, R, 4, 4, 2, 16, HALF), bf),
            vm((6, 32, 4, 8, 128), f32), vm((6, 32, 4, 8, 128), f32),
            vm((6, 32, 8, 128), f32), vm((6, 32, 8, 128), f32), vm((6, 32, 8, 128), f32),
            vm((2, 6, 256, 128), bf),
            vm((R, 256, 2 * F), bf),
            dma((16,)), dma((16,)), dma((8,)), dma((8,)), dma((1,)), dma((1,)),
            dma((4,)), dma((4,)), dma((4,)), dma((4,)), dma((4,)), dma((4,)),
            dma((2, R, 4)), dma((2, R, 4)), dma((2, R, 4)), dma((2, R, 4)),
        ],
        compiler_params=pltpu.CompilerParams(
            collective_id=1, has_side_effects=True, vmem_limit_bytes=56 * 2**20),
        name="whiten_correlate",
    )(block, limit, flags, spec, rows, cols, table)


def shards(spectra, window_flags, source_block, offset_limit):
    rows, cols, table = (jnp.asarray(v, jnp.bfloat16) for v in constants())
    spec = spectra.reshape(2, 256, F)
    out = fused(source_block, offset_limit, window_flags, spec, rows, cols, table)
    return out.reshape(R, 8, 32, 2 * F)


def solution(mesh):
    in_specs = (P(None, "chan", "win", None), P("win"), P(), P())
    out_specs = P(None, "win", "chan", None)
    return jax.shard_map(shards, mesh=mesh, in_specs=in_specs, out_specs=out_specs, check_vma=False)
```

```python
import math

import jax
import jax.numpy as jnp
import numpy as np
from jax import lax
from jax.experimental import pallas as pl
from jax.experimental.pallas import tpu as pltpu
from jax.sharding import PartitionSpec as P

MESH = pl.DeviceIdType.MESH
F = 768
HALF = 384
R = 4
SCALE = 1.0 / math.sqrt(24576.0)


def constants():
    rows = np.zeros((256, 256), np.float32)
    for wp in range(4):
        for p in range(4):
            for w2 in range(2):
                for c in range(8):
                    rows[((wp * 4 + p) * 2 + w2) * 8 + c, (p * 8 + c) * 8 + wp * 2 + w2] = 1.0
    cols = np.zeros((256, 256), np.float32)
    for i in range(128):
        cols[2 * i, i] = 1.0
        cols[2 * i + 1, 128 + i] = 1.0
    k = (256 * np.arange(3)[:, None] + 2 * np.arange(128)[None, :]).reshape(-1)
    lag = np.arange(768) - 768
    table = np.zeros((2, 768, 768), np.float32)
    for h in range(2):
        kk = k + h
        m = (kk[:, None] * lag[None, :]) % 1536
        g = np.where(kk == 0, 1.0, 2.0)[:, None]
        table[h, :HALF] = g * np.cos(np.pi * m / 768.0)
        table[h, HALF:] = -g * np.sin(np.pi * m / 768.0)
    return rows, cols, table


def coords():
    c, w = lax.axis_index("chan"), lax.axis_index("win")
    return c // 8, (c // 2) % 4, c % 2, w


def dev(x, z, yh, j):
    return (x * 8 + z * 2 + yh, j)


def whiten_into(spec_ref, flag_ref, rows_ref, cols_ref, out):
    for wp in range(4):
        part = []
        for reim in range(2):
            moved = jnp.dot(rows_ref[pl.ds(wp * 64, 64), :], spec_ref[reim], preferred_element_type=jnp.float32)
            moved = moved.astype(jnp.bfloat16)
            cut = [
                jnp.dot(moved[:, 256 * b:256 * b + 256], cols_ref[...], preferred_element_type=jnp.float32)
                for b in range(3)
            ]
            even = jnp.concatenate([c[:, :128] for c in cut], axis=1)
            odd = jnp.concatenate([c[:, 128:] for c in cut], axis=1)
            part.append((even, odd))
        (re0, re1), (im0, im1) = part
        p0 = re0 * re0 + im0 * im0
        p1 = re1 * re1 + im1 * im1
        level = (jnp.sum(p0, axis=1, keepdims=True) + jnp.sum(p1, axis=1, keepdims=True)) * (1.0 / F)
        base = 0.25 * level + 1e-06
        row = lax.broadcasted_iota(jnp.int32, (64, 1), 0)
        f0 = flag_ref[2 * wp].astype(jnp.float32)
        f1 = flag_ref[2 * wp + 1].astype(jnp.float32)
        flag = jnp.where((row // 8) % 2 == 0, f0, f1)
        q0 = lax.rsqrt(p0 + base) * flag
        q1 = lax.rsqrt(p1 + base) * flag
        for reim, h, v in ((0, 0, re0 * q0), (0, 1, re1 * q1), (1, 0, im0 * q0), (1, 1, im1 * q1)):
            v = v.astype(jnp.bfloat16).reshape(4, 16, HALF)
            for b in range(3):
                out[b, reim * 8 + wp * 2 + h] = v[:, :, 128 * b:128 * b + 128]


def spread_receivers(recv, b, xr, xi, xs):
    @pl.loop(0, 4)
    def _(a):
        for wp in range(4):
            n = a * 4 + wp
            for h in range(2):
                for p in range(4):
                    re = recv[a, b, wp * 2 + h, p].astype(jnp.float32)
                    im = recv[a, b, 8 + wp * 2 + h, p].astype(jnp.float32)
                    for w2 in range(2):
                        cut = slice(8 * w2, 8 * w2 + 8)
                        xr[h, n * 2 + w2, p] = re[cut]
                        xi[h, n * 2 + w2, p] = im[cut]
                        xs[h, n * 2 + w2, p] = re[cut] + im[cut]


def spread_sources(src, b, r, yr, yi, yd):
    for n in range(16):
        a, wp = n // 4, n % 4
        for h in range(2):
            lo, hi = wp * 2 + h, 8 + wp * 2 + h
            vr = src[b, a // 2, r, lo // 4, lo % 4, a % 2].astype(jnp.float32)
            vi = src[b, a // 2, r, hi // 4, hi % 4, a % 2].astype(jnp.float32)
            for w2 in range(2):
                cr = vr[8 * w2:8 * w2 + 8]
                ci = vi[8 * w2:8 * w2 + 8]
                yr[h, n * 2 + w2] = cr
                yi[h, n * 2 + w2] = ci
                yd[h, n * 2 + w2] = cr - ci


VMEM = 56 * 2**20
SB = 4
UNROLL = 8


def cross_round(xr, xi, xs, yr, yi, yd, stack, r, b, root, limit, chan, member):
    c8 = lax.broadcasted_iota(jnp.int32, (8, 1), 0)

    @pl.loop(0, 2)
    def _(h):
        for s0 in range(0, 8, SB):
            def step(w, acc):
                acc = list(acc)
                for u in range(UNROLL):
                    ww = w * UNROLL + u
                    ar = [xr[h, ww, p] for p in range(4)]
                    ai = [xi[h, ww, p] for p in range(4)]
                    asum = [xs[h, ww, p] for p in range(4)]
                    for s in range(SB):
                        br = jnp.broadcast_to(yr[h, ww, pl.ds(s0 + s, 1)], (8, 128))
                        bi = jnp.broadcast_to(yi[h, ww, pl.ds(s0 + s, 1)], (8, 128))
                        bd = jnp.broadcast_to(yd[h, ww, pl.ds(s0 + s, 1)], (8, 128))
                        for p in range(4):
                            i = (s * 4 + p) * 3
                            acc[i] = acc[i] + ar[p] * br
                            acc[i + 1] = acc[i + 1] + ai[p] * bi
                            acc[i + 2] = acc[i + 2] + asum[p] * bd
                return tuple(acc)

            zero = jnp.zeros((8, 128), jnp.float32)
            acc = lax.fori_loop(0, 32 // UNROLL, step, (zero,) * (SB * 12))
            for s in range(SB):
                sender = root * 32 + member * 8 + s0 + s
                re, im = [], []
                for p in range(4):
                    p1, p2, p3 = acc[(s * 4 + p) * 3:(s * 4 + p) * 3 + 3]
                    gap = jnp.abs(chan * 32 + p * 8 + c8 - sender)
                    keep = jnp.where((gap >= 1) & (gap <= limit), SCALE, 0.0)
                    re.append((p1 + p2) * keep)
                    im.append((p3 - p1 + p2) * keep)
                row = (s0 + s) * 32
                stack[b, r, h, 0, pl.ds(row, 32), :] = jnp.concatenate(re, axis=0).astype(jnp.bfloat16)
                stack[b, r, h, 1, pl.ds(row, 32), :] = jnp.concatenate(im, axis=0).astype(jnp.bfloat16)


def kernel(block_ref, limit_ref, flag_ref, spec_hbm, rows_hbm, cols_hbm, out_hbm,
           spec, rows, cols, recv, cand0, cand1, cand2, pick, diag0, diag1, diag2, src, xr, xi, xs, yr, yi, yd, stack,
           a_s, a_r, d_s, d_r, p_s, p_r, g_s, g_r, f_s, f_r, i_s, o_s, t_s, t_r, u_s, u_r):
    x, z, yh, j = coords()
    slot = x * 4 + z
    cand, diag = (cand0, cand1, cand2), (diag0, diag1, diag2)
    bar = pltpu.get_barrier_semaphore()
    plane = []
    for t in range(1, 16):
        to = (slot + t) % 16
        plane.append((to, dev(to // 4, to % 4, yh, j)))
    column = []
    for t in range(1, 8):
        column.append((t, (j + t) % 4, dev(x, z, (yh + t // 4) % 2, (j + t) % 4)))
    loads = [
        pltpu.make_async_copy(s, d, i_s.at[n])
        for n, (s, d) in enumerate(((spec_hbm, spec), (rows_hbm, rows), (cols_hbm, cols)))
    ]
    for c in loads:
        c.start()
    for _, d in plane:
        pl.semaphore_signal(bar, inc=1, device_id=d, device_id_type=MESH)
    for _, _, d in column:
        pl.semaphore_signal(bar, inc=1, device_id=d, device_id_type=MESH)

    for c in loads:
        c.wait()
    whiten_into(spec, flag_ref, rows, cols, recv.at[j])
    pl.semaphore_wait(bar, 22)
    sends = []

    def remote(s, d, ss, rs, to):
        return pltpu.make_async_remote_copy(
            src_ref=s, dst_ref=d, send_sem=ss, recv_sem=rs, device_id=to, device_id_type=MESH)

    def send(*args):
        c = remote(*args)
        c.start()
        sends.append(c)
        return c

    mate = dev(x, z, yh, j + 1 - 2 * (j % 2))
    across = (j + 2) % 4
    other = dev(x, z, yh, across)
    swap = []

    def exchange(b):
        swap.append([
            send(recv.at[j, b, to], cand[b].at[slot], a_s.at[b, t], a_r.at[b, t], d)
            for t, (to, d) in enumerate(plane)
        ])

    exchange(0)
    over = []

    def cross_over(b):
        over.append(send(recv.at[j, b], recv.at[j, b], g_s.at[b], g_r.at[b], other))

    cross_over(0)
    to_mate = [send(recv.at[j, b], recv.at[j, b], p_s.at[b], p_r.at[b], mate) for b in range(3)]
    for b in range(3):
        cand[b][slot] = recv[j, b, slot]

    def relay(b):
        over[b].wait_recv()
        return send(recv.at[across, b], recv.at[across, b], f_s.at[b], f_r.at[b], mate)

    def choose(b):
        for c in swap[b]:
            c.wait_recv()
        for r in range(R):
            pick[b, :, r] = cand[b][block_ref[r] // 2]
        diag[b][yh, j] = pick[b, j]
        return [send(pick.at[b, p], diag[b].at[yh, j], d_s.at[b, t], d_r.at[b, t], d) for t, p, d in column]

    def gather(b, meet):
        for c in meet:
            c.wait_recv()
        for r in range(R):
            got = diag[b][block_ref[r] % 2, :, r]
            src[b, 0, r, x, z] = got[0:2]
            src[b, 1, r, x, z] = got[2:4]
        out = []
        for d in range(1, 4):
            z2, x2 = (z + d) % 4, (x + d) % 4
            out.append(send(src.at[b, 0, :, x, z], src.at[b, 0, :, x, z], t_s.at[b, 0, d], t_r.at[b, 0, d], dev(x, z2, yh, j)))
            out.append(send(src.at[b, 1, :, x, z], src.at[b, 1, :, x, z], t_s.at[b, 1, d], t_r.at[b, 1, d], dev(x2, z, yh, j)))
        return out

    def spread(b, r, d):
        z2, x2 = (z + d) % 4, (x + d) % 4
        return (
            remote(src.at[b, 0, r, x], src.at[b, 0, r, x], u_s.at[b, 0, r, d], u_r.at[b, 0, r, d], dev(x2, z, yh, j)),
            remote(src.at[b, 1, r, :, z], src.at[b, 1, r, :, z], u_s.at[b, 1, r, d], u_r.at[b, 1, r, d], dev(x, z2, yh, j)),
        )

    def scatter(b, first, rounds):
        for c in first:
            c.wait_recv()
        for r in rounds:
            for d in range(1, 4):
                for c in spread(b, r, d):
                    c.start()

    chan = x * 8 + z * 2 + yh
    relayed = []

    def receivers(b):
        to_mate[b].wait_recv()
        relayed[b].wait_recv()
        spread_receivers(recv, b, xr, xi, xs)

    def arrived(b, r):
        for d in range(1, 4):
            for c in spread(b, r, d):
                c.wait_recv()

    def compute(b, r):
        spread_sources(src, b, r, yr, yi, yd)
        cross_round(xr, xi, xs, yr, yi, yd, stack, r, b, block_ref[r], limit_ref[r], chan, j)
        pltpu.make_async_copy(stack.at[b, r], out_hbm.at[b, r], o_s.at[b, r]).start()

    swap[0].pop(0).wait_recv()
    exchange(1)
    m0 = choose(0)
    exchange(2)
    cross_over(1)
    m1 = choose(1)
    f0 = gather(0, m0)
    cross_over(2)
    relayed.append(relay(0))
    m2 = choose(2)
    scatter(0, f0, (0, 1))
    f1 = gather(1, m1)
    f2 = gather(2, m2)
    relayed.append(relay(1))
    receivers(0)
    arrived(0, 0)
    scatter(0, (), (2, 3))
    compute(0, 0)
    scatter(1, f1, range(R))
    arrived(0, 1)
    compute(0, 1)
    scatter(2, f2, range(R))
    relayed.append(relay(2))

    @pl.loop(2, R)
    def _(r):
        arrived(0, r)
        compute(0, r)

    for b in (1, 2):
        receivers(b)

        @pl.loop(0, R)
        def _(r):
            arrived(b, r)
            compute(b, r)

    for r in range(R):
        for b in range(3):
            pltpu.make_async_copy(stack.at[b, r], out_hbm.at[b, r], o_s.at[b, r]).wait()
            for d in range(1, 4):
                for c in spread(b, r, d):
                    c.wait_send()
    for c in sends:
        c.wait_send()


def fused(block, limit, flags, spec, rows, cols):
    bf, f32 = jnp.bfloat16, jnp.float32
    dma = pltpu.SemaphoreType.DMA
    hbm = pl.BlockSpec(memory_space=pl.ANY)
    sm = pl.BlockSpec(memory_space=pltpu.SMEM)
    vm = pltpu.VMEM
    return pl.pallas_call(
        kernel,
        out_shape=jax.ShapeDtypeStruct((3, R, 2, 2, 256, 128), bf),
        in_specs=[sm, sm, sm, hbm, hbm, hbm],
        out_specs=hbm,
        scratch_shapes=[
            vm((2, 256, F), bf), vm((256, 256), bf), vm((256, 256), bf),
            vm((4, 3, 16, 4, 16, 128), bf),
            vm((16, 4, 16, 128), bf), vm((16, 4, 16, 128), bf), vm((16, 4, 16, 128), bf),
            vm((3, 4, R, 16, 128), bf),
            vm((2, 4, R, 16, 128), bf), vm((2, 4, R, 16, 128), bf), vm((2, 4, R, 16, 128), bf),
            vm((3, 2, R, 4, 4, 2, 16, 128), bf),
            vm((2, 32, 4, 8, 128), f32), vm((2, 32, 4, 8, 128), f32), vm((2, 32, 4, 8, 128), f32),
            vm((2, 32, 8, 128), f32), vm((2, 32, 8, 128), f32), vm((2, 32, 8, 128), f32),
            vm((3, R, 2, 2, 256, 128), bf),
            dma((3, 16)), dma((3, 16)), dma((3, 8)), dma((3, 8)), dma((3,)), dma((3,)),
            dma((3,)), dma((3,)), dma((3,)), dma((3,)), dma((3,)), dma((3, R)),
            dma((3, 2, 4)), dma((3, 2, 4)), dma((3, 2, R, 4)), dma((3, 2, R, 4)),
        ],
        compiler_params=pltpu.CompilerParams(
            collective_id=1, has_side_effects=True, vmem_limit_bytes=VMEM),
        name="whiten_correlate",
    )(block, limit, flags, spec, rows, cols)


def lag_kernel(stack, table, out):
    lhs = [jnp.concatenate([stack[b, 0, h, q] for q in range(2) for b in range(3)], axis=1) for h in range(2)]
    for n in range(3):
        cut = pl.ds(256 * n, 256)
        e = jnp.dot(lhs[0], table[0, :, cut], preferred_element_type=jnp.float32)
        o = jnp.dot(lhs[1], table[1, :, cut], preferred_element_type=jnp.float32)
        out[0, :, pl.ds(256 * n, 256)] = (e + o).astype(jnp.bfloat16)
        out[0, :, pl.ds(768 + 256 * n, 256)] = (e - o).astype(jnp.bfloat16)


def lags(stack, table):
    return pl.pallas_call(
        lag_kernel,
        grid=(R,),
        out_shape=jax.ShapeDtypeStruct((R, 256, 2 * F), jnp.bfloat16),
        in_specs=[
            pl.BlockSpec((3, 1, 2, 2, 256, 128), lambda r: (0, r, 0, 0, 0, 0)),
            pl.BlockSpec((2, F, F), lambda r: (0, 0, 0)),
        ],
        out_specs=pl.BlockSpec((1, 256, 2 * F), lambda r: (r, 0, 0)),
        compiler_params=pltpu.CompilerParams(vmem_limit_bytes=24 * 2**20),
        name="lag_product",
    )(stack, table)


def shards(spectra, window_flags, source_block, offset_limit):
    rows, cols, table = (jnp.asarray(v, jnp.bfloat16) for v in constants())
    spec = spectra.reshape(2, 256, F)
    stack = fused(source_block, offset_limit, window_flags, spec, rows, cols)
    out = lags(stack, table)
    return out.reshape(R, 8, 32, 2 * F)


def solution(mesh):
    in_specs = (P(None, "chan", "win", None), P("win"), P(), P())
    out_specs = P(None, "win", "chan", None)
    return jax.shard_map(shards, mesh=mesh, in_specs=in_specs, out_specs=out_specs, check_vma=False)
```

```python
import math

import jax
import jax.numpy as jnp
import numpy as np
from jax import lax
from jax.experimental import pallas as pl
from jax.experimental.pallas import tpu as pltpu
from jax.sharding import PartitionSpec as P

MESH = pl.DeviceIdType.MESH
F = 768
HALF = 384
R = 4
SCALE = 1.0 / math.sqrt(24576.0)


def constants():
    rows = np.zeros((256, 256), np.float32)
    for wp in range(4):
        for p in range(4):
            for w2 in range(2):
                for c in range(8):
                    rows[((wp * 4 + p) * 2 + w2) * 8 + c, (p * 8 + c) * 8 + wp * 2 + w2] = 1.0
    cols = np.zeros((256, 256), np.float32)
    for i in range(128):
        cols[2 * i, i] = 1.0
        cols[2 * i + 1, 128 + i] = 1.0
    k = (256 * np.arange(3)[:, None] + 2 * np.arange(128)[None, :]).reshape(-1)
    lag = np.arange(768) - 768
    table = np.zeros((2, 768, 768), np.float32)
    for h in range(2):
        kk = k + h
        m = (kk[:, None] * lag[None, :]) % 1536
        g = np.where(kk == 0, 1.0, 2.0)[:, None]
        table[h, :HALF] = g * np.cos(np.pi * m / 768.0)
        table[h, HALF:] = -g * np.sin(np.pi * m / 768.0)
    return rows, cols, table


def coords():
    c, w = lax.axis_index("chan"), lax.axis_index("win")
    return c // 8, (c // 2) % 4, c % 2, w


def dev(x, z, yh, j):
    return (x * 8 + z * 2 + yh, j)


def whiten_into(spec_ref, flag_ref, rows_ref, cols_ref, out):
    for wp in range(4):
        part = []
        for reim in range(2):
            moved = jnp.dot(rows_ref[pl.ds(wp * 64, 64), :], spec_ref[reim], preferred_element_type=jnp.float32)
            moved = moved.astype(jnp.bfloat16)
            cut = [
                jnp.dot(moved[:, 256 * b:256 * b + 256], cols_ref[...], preferred_element_type=jnp.float32)
                for b in range(3)
            ]
            even = jnp.concatenate([c[:, :128] for c in cut], axis=1)
            odd = jnp.concatenate([c[:, 128:] for c in cut], axis=1)
            part.append((even, odd))
        (re0, re1), (im0, im1) = part
        p0 = re0 * re0 + im0 * im0
        p1 = re1 * re1 + im1 * im1
        level = (jnp.sum(p0, axis=1, keepdims=True) + jnp.sum(p1, axis=1, keepdims=True)) * (1.0 / F)
        base = 0.25 * level + 1e-06
        row = lax.broadcasted_iota(jnp.int32, (64, 1), 0)
        f0 = flag_ref[2 * wp].astype(jnp.float32)
        f1 = flag_ref[2 * wp + 1].astype(jnp.float32)
        flag = jnp.where((row // 8) % 2 == 0, f0, f1)
        q0 = lax.rsqrt(p0 + base) * flag
        q1 = lax.rsqrt(p1 + base) * flag
        for reim, h, v in ((0, 0, re0 * q0), (0, 1, re1 * q1), (1, 0, im0 * q0), (1, 1, im1 * q1)):
            v = v.astype(jnp.bfloat16).reshape(4, 16, HALF)
            for b in range(3):
                out[b, reim * 8 + wp * 2 + h] = v[:, :, 128 * b:128 * b + 128]


def spread_receivers(recv, b, xr, xi, xs):
    @pl.loop(0, 4)
    def _(a):
        for wp in range(4):
            n = a * 4 + wp
            for h in range(2):
                for p in range(4):
                    re = recv[a, b, wp * 2 + h, p].astype(jnp.float32)
                    im = recv[a, b, 8 + wp * 2 + h, p].astype(jnp.float32)
                    for w2 in range(2):
                        cut = slice(8 * w2, 8 * w2 + 8)
                        xr[h, n * 2 + w2, p] = re[cut]
                        xi[h, n * 2 + w2, p] = im[cut]
                        xs[h, n * 2 + w2, p] = re[cut] + im[cut]


def spread_sources(src, b, r, yr, yi, yd):
    for n in range(16):
        a, wp = n // 4, n % 4
        for h in range(2):
            lo, hi = wp * 2 + h, 8 + wp * 2 + h
            vr = src[b, a // 2, r, lo // 4, lo % 4, a % 2].astype(jnp.float32)
            vi = src[b, a // 2, r, hi // 4, hi % 4, a % 2].astype(jnp.float32)
            for w2 in range(2):
                cr = vr[8 * w2:8 * w2 + 8]
                ci = vi[8 * w2:8 * w2 + 8]
                yr[h, n * 2 + w2] = cr
                yi[h, n * 2 + w2] = ci
                yd[h, n * 2 + w2] = cr - ci


VMEM = 56 * 2**20
SB = 4
UNROLL = 32


def cross_round(xr, xi, xs, yr, yi, yd, stack, r, b, root, limit, chan, member):
    c8 = lax.broadcasted_iota(jnp.int32, (8, 1), 0)

    @pl.loop(0, 2)
    def _(h):
        for s0 in range(0, 8, SB):
            def step(w, acc):
                acc = list(acc)
                for u in range(UNROLL):
                    ww = w * UNROLL + u
                    ar = [xr[h, ww, p] for p in range(4)]
                    ai = [xi[h, ww, p] for p in range(4)]
                    asum = [xs[h, ww, p] for p in range(4)]
                    for s in range(SB):
                        br = jnp.broadcast_to(yr[h, ww, pl.ds(s0 + s, 1)], (8, 128))
                        bi = jnp.broadcast_to(yi[h, ww, pl.ds(s0 + s, 1)], (8, 128))
                        bd = jnp.broadcast_to(yd[h, ww, pl.ds(s0 + s, 1)], (8, 128))
                        for p in range(4):
                            i = (s * 4 + p) * 3
                            acc[i] = acc[i] + ar[p] * br
                            acc[i + 1] = acc[i + 1] + ai[p] * bi
                            acc[i + 2] = acc[i + 2] + asum[p] * bd
                return tuple(acc)

            zero = jnp.zeros((8, 128), jnp.float32)
            acc = lax.fori_loop(0, 32 // UNROLL, step, (zero,) * (SB * 12))
            for s in range(SB):
                sender = root * 32 + member * 8 + s0 + s
                re, im = [], []
                for p in range(4):
                    p1, p2, p3 = acc[(s * 4 + p) * 3:(s * 4 + p) * 3 + 3]
                    gap = jnp.abs(chan * 32 + p * 8 + c8 - sender)
                    keep = jnp.where((gap >= 1) & (gap <= limit), SCALE, 0.0)
                    re.append((p1 + p2) * keep)
                    im.append((p3 - p1 + p2) * keep)
                row = (s0 + s) * 32
                stack[b, r, h, 0, pl.ds(row, 32), :] = jnp.concatenate(re, axis=0).astype(jnp.bfloat16)
                stack[b, r, h, 1, pl.ds(row, 32), :] = jnp.concatenate(im, axis=0).astype(jnp.bfloat16)


def kernel(block_ref, limit_ref, flag_ref, spec_hbm, rows_hbm, cols_hbm, out_hbm,
           spec, rows, cols, recv, cand0, cand1, cand2, pick, diag0, diag1, diag2, src, xr, xi, xs, yr, yi, yd, stack,
           a_s, a_r, d_s, d_r, p_s, p_r, g_s, g_r, f_s, f_r, i_s, o_s, t_s, t_r, u_s, u_r):
    x, z, yh, j = coords()
    slot = x * 4 + z
    cand, diag = (cand0, cand1, cand2), (diag0, diag1, diag2)
    bar = pltpu.get_barrier_semaphore()
    plane = []
    for t in range(1, 16):
        to = (slot + t) % 16
        plane.append((to, dev(to // 4, to % 4, yh, j)))
    column = []
    for t in range(1, 8):
        column.append((t, (j + t) % 4, dev(x, z, (yh + t // 4) % 2, (j + t) % 4)))
    loads = [
        pltpu.make_async_copy(s, d, i_s.at[n])
        for n, (s, d) in enumerate(((spec_hbm, spec), (rows_hbm, rows), (cols_hbm, cols)))
    ]
    for c in loads:
        c.start()
    for _, d in plane:
        pl.semaphore_signal(bar, inc=1, device_id=d, device_id_type=MESH)
    for _, _, d in column:
        pl.semaphore_signal(bar, inc=1, device_id=d, device_id_type=MESH)

    for c in loads:
        c.wait()
    whiten_into(spec, flag_ref, rows, cols, recv.at[j])
    pl.semaphore_wait(bar, 22)
    sends = []

    def remote(s, d, ss, rs, to):
        return pltpu.make_async_remote_copy(
            src_ref=s, dst_ref=d, send_sem=ss, recv_sem=rs, device_id=to, device_id_type=MESH)

    def send(*args):
        c = remote(*args)
        c.start()
        sends.append(c)
        return c

    mate = dev(x, z, yh, j + 1 - 2 * (j % 2))
    across = (j + 2) % 4
    other = dev(x, z, yh, across)
    swap = []

    def exchange(b):
        swap.append([
            send(recv.at[j, b, to], cand[b].at[slot], a_s.at[b, t], a_r.at[b, t], d)
            for t, (to, d) in enumerate(plane)
        ])

    exchange(0)
    over = []

    def cross_over(b):
        over.append(send(recv.at[j, b], recv.at[j, b], g_s.at[b], g_r.at[b], other))

    cross_over(0)
    to_mate = [send(recv.at[j, b], recv.at[j, b], p_s.at[b], p_r.at[b], mate) for b in range(3)]
    for b in range(3):
        cand[b][slot] = recv[j, b, slot]

    def relay(b):
        over[b].wait_recv()
        return send(recv.at[across, b], recv.at[across, b], f_s.at[b], f_r.at[b], mate)

    def choose(b):
        for c in swap[b]:
            c.wait_recv()
        for r in range(R):
            pick[b, :, r] = cand[b][block_ref[r] // 2]
        diag[b][yh, j] = pick[b, j]
        return [send(pick.at[b, p], diag[b].at[yh, j], d_s.at[b, t], d_r.at[b, t], d) for t, p, d in column]

    def gather(b, meet):
        for c in meet:
            c.wait_recv()
        for r in range(R):
            got = diag[b][block_ref[r] % 2, :, r]
            src[b, 0, r, x, z] = got[0:2]
            src[b, 1, r, x, z] = got[2:4]
        out = []
        for d in range(1, 4):
            z2, x2 = (z + d) % 4, (x + d) % 4
            out.append(send(src.at[b, 0, :, x, z], src.at[b, 0, :, x, z], t_s.at[b, 0, d], t_r.at[b, 0, d], dev(x, z2, yh, j)))
            out.append(send(src.at[b, 1, :, x, z], src.at[b, 1, :, x, z], t_s.at[b, 1, d], t_r.at[b, 1, d], dev(x2, z, yh, j)))
        return out

    def spread(b, r, d):
        z2, x2 = (z + d) % 4, (x + d) % 4
        return (
            remote(src.at[b, 0, r, x], src.at[b, 0, r, x], u_s.at[b, 0, r, d], u_r.at[b, 0, r, d], dev(x2, z, yh, j)),
            remote(src.at[b, 1, r, :, z], src.at[b, 1, r, :, z], u_s.at[b, 1, r, d], u_r.at[b, 1, r, d], dev(x, z2, yh, j)),
        )

    def scatter(b, first, rounds):
        for c in first:
            c.wait_recv()
        for r in rounds:
            for d in range(1, 4):
                for c in spread(b, r, d):
                    c.start()

    chan = x * 8 + z * 2 + yh
    relayed = []

    def receivers(b):
        to_mate[b].wait_recv()
        relayed[b].wait_recv()
        spread_receivers(recv, b, xr, xi, xs)

    def arrived(b, r):
        for d in range(1, 4):
            for c in spread(b, r, d):
                c.wait_recv()

    def compute(b, r):
        spread_sources(src, b, r, yr, yi, yd)
        cross_round(xr, xi, xs, yr, yi, yd, stack, r, b, block_ref[r], limit_ref[r], chan, j)
        pltpu.make_async_copy(stack.at[b, r], out_hbm.at[b, r], o_s.at[b, r]).start()

    swap[0].pop(0).wait_recv()
    exchange(1)
    m0 = choose(0)
    exchange(2)
    cross_over(1)
    m1 = choose(1)
    f0 = gather(0, m0)
    cross_over(2)
    relayed.append(relay(0))
    m2 = choose(2)
    scatter(0, f0, (0, 1))
    f1 = gather(1, m1)
    f2 = gather(2, m2)
    relayed.append(relay(1))
    receivers(0)
    arrived(0, 0)
    scatter(0, (), (2, 3))
    compute(0, 0)
    scatter(1, f1, range(R))
    arrived(0, 1)
    compute(0, 1)
    scatter(2, f2, range(R))
    relayed.append(relay(2))

    @pl.loop(2, R)
    def _(r):
        arrived(0, r)
        compute(0, r)

    for b in (1, 2):
        receivers(b)

        @pl.loop(0, R)
        def _(r):
            arrived(b, r)
            compute(b, r)

    for r in range(R):
        for b in range(3):
            pltpu.make_async_copy(stack.at[b, r], out_hbm.at[b, r], o_s.at[b, r]).wait()
            for d in range(1, 4):
                for c in spread(b, r, d):
                    c.wait_send()
    for c in sends:
        c.wait_send()


def fused(block, limit, flags, spec, rows, cols):
    bf, f32 = jnp.bfloat16, jnp.float32
    dma = pltpu.SemaphoreType.DMA
    hbm = pl.BlockSpec(memory_space=pl.ANY)
    sm = pl.BlockSpec(memory_space=pltpu.SMEM)
    vm = pltpu.VMEM
    return pl.pallas_call(
        kernel,
        out_shape=jax.ShapeDtypeStruct((3, R, 2, 2, 256, 128), bf),
        in_specs=[sm, sm, sm, hbm, hbm, hbm],
        out_specs=hbm,
        scratch_shapes=[
            vm((2, 256, F), bf), vm((256, 256), bf), vm((256, 256), bf),
            vm((4, 3, 16, 4, 16, 128), bf),
            vm((16, 4, 16, 128), bf), vm((16, 4, 16, 128), bf), vm((16, 4, 16, 128), bf),
            vm((3, 4, R, 16, 128), bf),
            vm((2, 4, R, 16, 128), bf), vm((2, 4, R, 16, 128), bf), vm((2, 4, R, 16, 128), bf),
            vm((3, 2, R, 4, 4, 2, 16, 128), bf),
            vm((2, 32, 4, 8, 128), f32), vm((2, 32, 4, 8, 128), f32), vm((2, 32, 4, 8, 128), f32),
            vm((2, 32, 8, 128), f32), vm((2, 32, 8, 128), f32), vm((2, 32, 8, 128), f32),
            vm((3, R, 2, 2, 256, 128), bf),
            dma((3, 16)), dma((3, 16)), dma((3, 8)), dma((3, 8)), dma((3,)), dma((3,)),
            dma((3,)), dma((3,)), dma((3,)), dma((3,)), dma((3,)), dma((3, R)),
            dma((3, 2, 4)), dma((3, 2, 4)), dma((3, 2, R, 4)), dma((3, 2, R, 4)),
        ],
        compiler_params=pltpu.CompilerParams(
            collective_id=1, has_side_effects=True, vmem_limit_bytes=VMEM),
        name="whiten_correlate",
    )(block, limit, flags, spec, rows, cols)


def lag_kernel(stack_hbm, table_hbm, out_hbm, stack, table, out, s_sem, t_sem, o_sem):
    takes = [pltpu.make_async_copy(stack_hbm.at[:, r], stack.at[r], s_sem.at[r]) for r in range(R)]
    cols = [
        pltpu.make_async_copy(table_hbm.at[:, :, pl.ds(256 * n, 256)], table.at[n], t_sem.at[n]) for n in range(3)
    ]
    takes[0].start()
    for c in cols:
        c.start()
    for c in takes[1:]:
        c.start()
    puts = []
    for r in range(R):
        takes[r].wait()
        lhs = [jnp.concatenate([stack[r, b, h, q] for q in range(2) for b in range(3)], axis=1) for h in range(2)]
        for n in range(3):
            if r == 0:
                cols[n].wait()
            e = jnp.dot(lhs[0], table[n, 0], preferred_element_type=jnp.float32)
            o = jnp.dot(lhs[1], table[n, 1], preferred_element_type=jnp.float32)
            out[r, :, pl.ds(256 * n, 256)] = (e + o).astype(jnp.bfloat16)
            out[r, :, pl.ds(768 + 256 * n, 256)] = (e - o).astype(jnp.bfloat16)
        puts.append(pltpu.make_async_copy(out.at[r], out_hbm.at[r], o_sem.at[r]))
        puts[-1].start()
    for c in puts:
        c.wait()


def lags(stack, table):
    bf, dma = jnp.bfloat16, pltpu.SemaphoreType.DMA
    hbm = pl.BlockSpec(memory_space=pl.ANY)
    return pl.pallas_call(
        lag_kernel,
        out_shape=jax.ShapeDtypeStruct((R, 256, 2 * F), bf),
        in_specs=[hbm, hbm],
        out_specs=hbm,
        scratch_shapes=[
            pltpu.VMEM((R, 3, 2, 2, 256, 128), bf),
            pltpu.VMEM((3, 2, F, 256), bf),
            pltpu.VMEM((R, 256, 2 * F), bf),
            dma((R,)), dma((3,)), dma((R,)),
        ],
        compiler_params=pltpu.CompilerParams(vmem_limit_bytes=60 * 2**20),
        name="lag_product",
    )(stack, table)


def shards(spectra, window_flags, source_block, offset_limit):
    rows, cols, table = (jnp.asarray(v, jnp.bfloat16) for v in constants())
    spec = spectra.reshape(2, 256, F)
    stack = fused(source_block, offset_limit, window_flags, spec, rows, cols)
    out = lags(stack, table)
    return out.reshape(R, 8, 32, 2 * F)


def solution(mesh):
    in_specs = (P(None, "chan", "win", None), P("win"), P(), P())
    out_specs = P(None, "win", "chan", None)
    return jax.shard_map(shards, mesh=mesh, in_specs=in_specs, out_specs=out_specs, check_vma=False)
```

```python
import math

import jax
import jax.numpy as jnp
import numpy as np
from jax import lax
from jax.experimental import pallas as pl
from jax.experimental.pallas import tpu as pltpu
from jax.sharding import PartitionSpec as P

MESH = pl.DeviceIdType.MESH
F = 768
HALF = 384
R = 4
SCALE = 1.0 / math.sqrt(24576.0)


def constants():
    rows = np.zeros((256, 256), np.float32)
    for wp in range(4):
        for p in range(4):
            for w2 in range(2):
                for c in range(8):
                    rows[((wp * 4 + p) * 2 + w2) * 8 + c, (p * 8 + c) * 8 + wp * 2 + w2] = 1.0
    cols = np.zeros((256, 256), np.float32)
    for i in range(128):
        cols[2 * i, i] = 1.0
        cols[2 * i + 1, 128 + i] = 1.0
    k = (256 * np.arange(3)[:, None] + 2 * np.arange(128)[None, :]).reshape(-1)
    lag = np.arange(768) - 768
    table = np.zeros((2, 768, 768), np.float32)
    for h in range(2):
        kk = k + h
        m = (kk[:, None] * lag[None, :]) % 1536
        g = np.where(kk == 0, 1.0, 2.0)[:, None]
        table[h, :HALF] = g * np.cos(np.pi * m / 768.0)
        table[h, HALF:] = -g * np.sin(np.pi * m / 768.0)
    return rows, cols, table


def coords():
    c, w = lax.axis_index("chan"), lax.axis_index("win")
    return c // 8, (c // 2) % 4, c % 2, w


def dev(x, z, yh, j):
    return (x * 8 + z * 2 + yh, j)


def whiten_into(spec_ref, flag_ref, rows_ref, cols_ref, out):
    whole = []
    for reim in range(2):
        moved = jnp.dot(rows_ref[...], spec_ref[reim], preferred_element_type=jnp.float32).astype(jnp.bfloat16)
        cut = [
            jnp.dot(moved[:, 256 * b:256 * b + 256], cols_ref[...], preferred_element_type=jnp.float32)
            for b in range(3)
        ]
        whole.append([jnp.concatenate([c[:, 128 * h:128 * h + 128] for c in cut], axis=1) for h in range(2)])
    for wp in range(4):
        part = [[v[64 * wp:64 * wp + 64] for v in pair] for pair in whole]
        (re0, re1), (im0, im1) = part
        p0 = re0 * re0 + im0 * im0
        p1 = re1 * re1 + im1 * im1
        level = (jnp.sum(p0, axis=1, keepdims=True) + jnp.sum(p1, axis=1, keepdims=True)) * (1.0 / F)
        base = 0.25 * level + 1e-06
        row = lax.broadcasted_iota(jnp.int32, (64, 1), 0)
        f0 = flag_ref[2 * wp].astype(jnp.float32)
        f1 = flag_ref[2 * wp + 1].astype(jnp.float32)
        flag = jnp.where((row // 8) % 2 == 0, f0, f1)
        q0 = lax.rsqrt(p0 + base) * flag
        q1 = lax.rsqrt(p1 + base) * flag
        for reim, h, v in ((0, 0, re0 * q0), (0, 1, re1 * q1), (1, 0, im0 * q0), (1, 1, im1 * q1)):
            v = v.astype(jnp.bfloat16).reshape(4, 16, HALF)
            for b in range(3):
                out[b, reim * 8 + wp * 2 + h] = v[:, :, 128 * b:128 * b + 128]


def spread_receivers(recv, b, xr, xi, xs):
    @pl.loop(0, 4)
    def _(a):
        for wp in range(4):
            n = a * 4 + wp
            for h in range(2):
                for p in range(4):
                    re = recv[a, b, wp * 2 + h, p].astype(jnp.float32)
                    im = recv[a, b, 8 + wp * 2 + h, p].astype(jnp.float32)
                    for w2 in range(2):
                        cut = slice(8 * w2, 8 * w2 + 8)
                        xr[h, n * 2 + w2, p] = re[cut]
                        xi[h, n * 2 + w2, p] = im[cut]
                        xs[h, n * 2 + w2, p] = re[cut] + im[cut]


def spread_sources(src, b, r, yr, yi, yd):
    for n in range(16):
        a, wp = n // 4, n % 4
        for h in range(2):
            lo, hi = wp * 2 + h, 8 + wp * 2 + h
            vr = src[b, a // 2, r, lo // 4, lo % 4, a % 2].astype(jnp.float32)
            vi = src[b, a // 2, r, hi // 4, hi % 4, a % 2].astype(jnp.float32)
            for w2 in range(2):
                cr = vr[8 * w2:8 * w2 + 8]
                ci = vi[8 * w2:8 * w2 + 8]
                yr[h, n * 2 + w2] = cr
                yi[h, n * 2 + w2] = ci
                yd[h, n * 2 + w2] = cr - ci


VMEM = 56 * 2**20
SB = 4
UNROLL = 32


def cross_round(xr, xi, xs, yr, yi, yd, stack, r, b, root, limit, chan, member):
    c8 = lax.broadcasted_iota(jnp.int32, (8, 1), 0)

    @pl.loop(0, 2)
    def _(h):
        for s0 in range(0, 8, SB):
            def step(w, acc):
                acc = list(acc)
                for u in range(UNROLL):
                    ww = w * UNROLL + u
                    ar = [xr[h, ww, p] for p in range(4)]
                    ai = [xi[h, ww, p] for p in range(4)]
                    asum = [xs[h, ww, p] for p in range(4)]
                    for s in range(SB):
                        br = jnp.broadcast_to(yr[h, ww, pl.ds(s0 + s, 1)], (8, 128))
                        bi = jnp.broadcast_to(yi[h, ww, pl.ds(s0 + s, 1)], (8, 128))
                        bd = jnp.broadcast_to(yd[h, ww, pl.ds(s0 + s, 1)], (8, 128))
                        for p in range(4):
                            i = (s * 4 + p) * 3
                            acc[i] = acc[i] + ar[p] * br
                            acc[i + 1] = acc[i + 1] + ai[p] * bi
                            acc[i + 2] = acc[i + 2] + asum[p] * bd
                return tuple(acc)

            zero = jnp.zeros((8, 128), jnp.float32)
            acc = lax.fori_loop(0, 32 // UNROLL, step, (zero,) * (SB * 12))
            for s in range(SB):
                sender = root * 32 + member * 8 + s0 + s
                re, im = [], []
                for p in range(4):
                    p1, p2, p3 = acc[(s * 4 + p) * 3:(s * 4 + p) * 3 + 3]
                    gap = jnp.abs(chan * 32 + p * 8 + c8 - sender)
                    keep = jnp.where((gap >= 1) & (gap <= limit), SCALE, 0.0)
                    re.append((p1 + p2) * keep)
                    im.append((p3 - p1 + p2) * keep)
                row = (s0 + s) * 32
                stack[b, r, h, 0, pl.ds(row, 32), :] = jnp.concatenate(re, axis=0).astype(jnp.bfloat16)
                stack[b, r, h, 1, pl.ds(row, 32), :] = jnp.concatenate(im, axis=0).astype(jnp.bfloat16)


def kernel(block_ref, limit_ref, flag_ref, spec_hbm, rows_hbm, cols_hbm, out_hbm,
           spec, rows, cols, recv, cand0, cand1, cand2, pick, diag0, diag1, diag2, src, xr, xi, xs, yr, yi, yd, stack,
           a_s, a_r, d_s, d_r, p_s, p_r, g_s, g_r, f_s, f_r, i_s, o_s, t_s, t_r, u_s, u_r):
    x, z, yh, j = coords()
    slot = x * 4 + z
    cand, diag = (cand0, cand1, cand2), (diag0, diag1, diag2)
    bar = pltpu.get_barrier_semaphore()
    plane = []
    for t in range(1, 16):
        to = (slot + t) % 16
        plane.append((to, dev(to // 4, to % 4, yh, j)))
    column = []
    for t in range(1, 8):
        column.append((t, (j + t) % 4, dev(x, z, (yh + t // 4) % 2, (j + t) % 4)))
    loads = [
        pltpu.make_async_copy(s, d, i_s.at[n])
        for n, (s, d) in enumerate(((spec_hbm, spec), (rows_hbm, rows), (cols_hbm, cols)))
    ]
    for c in loads:
        c.start()
    for _, d in plane:
        pl.semaphore_signal(bar, inc=1, device_id=d, device_id_type=MESH)
    for _, _, d in column:
        pl.semaphore_signal(bar, inc=1, device_id=d, device_id_type=MESH)

    for c in loads:
        c.wait()
    whiten_into(spec, flag_ref, rows, cols, recv.at[j])
    pl.semaphore_wait(bar, 22)
    sends = []

    def remote(s, d, ss, rs, to):
        return pltpu.make_async_remote_copy(
            src_ref=s, dst_ref=d, send_sem=ss, recv_sem=rs, device_id=to, device_id_type=MESH)

    def send(*args):
        c = remote(*args)
        c.start()
        sends.append(c)
        return c

    mate = dev(x, z, yh, j + 1 - 2 * (j % 2))
    across = (j + 2) % 4
    other = dev(x, z, yh, across)
    swap = []

    def exchange(b):
        swap.append([
            send(recv.at[j, b, to], cand[b].at[slot], a_s.at[b, t], a_r.at[b, t], d)
            for t, (to, d) in enumerate(plane)
        ])

    exchange(0)
    over = []

    def cross_over(b):
        over.append(send(recv.at[j, b], recv.at[j, b], g_s.at[b], g_r.at[b], other))

    cross_over(0)
    to_mate = [send(recv.at[j, b], recv.at[j, b], p_s.at[b], p_r.at[b], mate) for b in range(3)]
    for b in range(3):
        cand[b][slot] = recv[j, b, slot]

    def relay(b):
        over[b].wait_recv()
        return send(recv.at[across, b], recv.at[across, b], f_s.at[b], f_r.at[b], mate)

    def choose(b):
        for c in swap[b]:
            c.wait_recv()
        for r in range(R):
            pick[b, :, r] = cand[b][block_ref[r] // 2]
        diag[b][yh, j] = pick[b, j]
        return [send(pick.at[b, p], diag[b].at[yh, j], d_s.at[b, t], d_r.at[b, t], d) for t, p, d in column]

    def gather(b, meet):
        for c in meet:
            c.wait_recv()
        for r in range(R):
            got = diag[b][block_ref[r] % 2, :, r]
            src[b, 0, r, x, z] = got[0:2]
            src[b, 1, r, x, z] = got[2:4]
        out = []
        for d in range(1, 4):
            z2, x2 = (z + d) % 4, (x + d) % 4
            out.append(send(src.at[b, 0, :, x, z], src.at[b, 0, :, x, z], t_s.at[b, 0, d], t_r.at[b, 0, d], dev(x, z2, yh, j)))
            out.append(send(src.at[b, 1, :, x, z], src.at[b, 1, :, x, z], t_s.at[b, 1, d], t_r.at[b, 1, d], dev(x2, z, yh, j)))
        return out

    def spread(b, r, d):
        z2, x2 = (z + d) % 4, (x + d) % 4
        return (
            remote(src.at[b, 0, r, x], src.at[b, 0, r, x], u_s.at[b, 0, r, d], u_r.at[b, 0, r, d], dev(x2, z, yh, j)),
            remote(src.at[b, 1, r, :, z], src.at[b, 1, r, :, z], u_s.at[b, 1, r, d], u_r.at[b, 1, r, d], dev(x, z2, yh, j)),
        )

    def scatter(b, first, rounds):
        for c in first:
            c.wait_recv()
        for r in rounds:
            for d in range(1, 4):
                for c in spread(b, r, d):
                    c.start()

    chan = x * 8 + z * 2 + yh
    relayed = []

    def receivers(b):
        to_mate[b].wait_recv()
        relayed[b].wait_recv()
        spread_receivers(recv, b, xr, xi, xs)

    def arrived(b, r):
        for d in range(1, 4):
            for c in spread(b, r, d):
                c.wait_recv()

    def compute(b, r):
        spread_sources(src, b, r, yr, yi, yd)
        cross_round(xr, xi, xs, yr, yi, yd, stack, r, b, block_ref[r], limit_ref[r], chan, j)
        pltpu.make_async_copy(stack.at[b, r], out_hbm.at[b, r], o_s.at[b, r]).start()

    swap[0].pop(0).wait_recv()
    exchange(1)
    m0 = choose(0)
    exchange(2)
    m1 = choose(1)
    cross_over(1)
    f0 = gather(0, m0)
    relayed.append(relay(0))
    m2 = choose(2)
    cross_over(2)
    scatter(0, f0, range(R))
    f1 = gather(1, m1)
    f2 = gather(2, m2)
    receivers(0)
    arrived(0, 0)
    compute(0, 0)
    scatter(1, f1, range(R))
    relayed.append(relay(1))
    arrived(0, 1)
    compute(0, 1)
    scatter(2, f2, range(R))
    relayed.append(relay(2))

    @pl.loop(2, R)
    def _(r):
        arrived(0, r)
        compute(0, r)

    for b in (1, 2):
        receivers(b)

        @pl.loop(0, R)
        def _(r):
            arrived(b, r)
            compute(b, r)

    for r in range(R):
        for b in range(3):
            pltpu.make_async_copy(stack.at[b, r], out_hbm.at[b, r], o_s.at[b, r]).wait()
            for d in range(1, 4):
                for c in spread(b, r, d):
                    c.wait_send()
    for c in sends:
        c.wait_send()


def fused(block, limit, flags, spec, rows, cols):
    bf, f32 = jnp.bfloat16, jnp.float32
    dma = pltpu.SemaphoreType.DMA
    hbm = pl.BlockSpec(memory_space=pl.ANY)
    sm = pl.BlockSpec(memory_space=pltpu.SMEM)
    vm = pltpu.VMEM
    return pl.pallas_call(
        kernel,
        out_shape=jax.ShapeDtypeStruct((3, R, 2, 2, 256, 128), bf),
        in_specs=[sm, sm, sm, hbm, hbm, hbm],
        out_specs=hbm,
        scratch_shapes=[
            vm((2, 256, F), bf), vm((256, 256), bf), vm((256, 256), bf),
            vm((4, 3, 16, 4, 16, 128), bf),
            vm((16, 4, 16, 128), bf), vm((16, 4, 16, 128), bf), vm((16, 4, 16, 128), bf),
            vm((3, 4, R, 16, 128), bf),
            vm((2, 4, R, 16, 128), bf), vm((2, 4, R, 16, 128), bf), vm((2, 4, R, 16, 128), bf),
            vm((3, 2, R, 4, 4, 2, 16, 128), bf),
            vm((2, 32, 4, 8, 128), f32), vm((2, 32, 4, 8, 128), f32), vm((2, 32, 4, 8, 128), f32),
            vm((2, 32, 8, 128), f32), vm((2, 32, 8, 128), f32), vm((2, 32, 8, 128), f32),
            vm((3, R, 2, 2, 256, 128), bf),
            dma((3, 16)), dma((3, 16)), dma((3, 8)), dma((3, 8)), dma((3,)), dma((3,)),
            dma((3,)), dma((3,)), dma((3,)), dma((3,)), dma((3,)), dma((3, R)),
            dma((3, 2, 4)), dma((3, 2, 4)), dma((3, 2, R, 4)), dma((3, 2, R, 4)),
        ],
        compiler_params=pltpu.CompilerParams(
            collective_id=1, has_side_effects=True, vmem_limit_bytes=VMEM),
        name="whiten_correlate",
    )(block, limit, flags, spec, rows, cols)


def lag_kernel(stack_hbm, table_hbm, out_hbm, stack, table, out, s_sem, t_sem, o_sem):
    takes = [pltpu.make_async_copy(stack_hbm.at[:, r], stack.at[r], s_sem.at[r]) for r in range(R)]
    cols = [
        pltpu.make_async_copy(table_hbm.at[:, :, pl.ds(256 * n, 256)], table.at[n], t_sem.at[n]) for n in range(3)
    ]
    takes[0].start()
    for c in cols:
        c.start()
    for c in takes[1:]:
        c.start()
    puts = []
    for r in range(R):
        takes[r].wait()
        lhs = [jnp.concatenate([stack[r, b, h, q] for q in range(2) for b in range(3)], axis=1) for h in range(2)]
        for n in range(3):
            if r == 0:
                cols[n].wait()
            e = jnp.dot(lhs[0], table[n, 0], preferred_element_type=jnp.float32)
            o = jnp.dot(lhs[1], table[n, 1], preferred_element_type=jnp.float32)
            out[r, :, pl.ds(256 * n, 256)] = (e + o).astype(jnp.bfloat16)
            out[r, :, pl.ds(768 + 256 * n, 256)] = (e - o).astype(jnp.bfloat16)
        puts.append(pltpu.make_async_copy(out.at[r], out_hbm.at[r], o_sem.at[r]))
        puts[-1].start()
    for c in puts:
        c.wait()


def lags(stack, table):
    bf, dma = jnp.bfloat16, pltpu.SemaphoreType.DMA
    hbm = pl.BlockSpec(memory_space=pl.ANY)
    return pl.pallas_call(
        lag_kernel,
        out_shape=jax.ShapeDtypeStruct((R, 256, 2 * F), bf),
        in_specs=[hbm, hbm],
        out_specs=hbm,
        scratch_shapes=[
            pltpu.VMEM((R, 3, 2, 2, 256, 128), bf),
            pltpu.VMEM((3, 2, F, 256), bf),
            pltpu.VMEM((R, 256, 2 * F), bf),
            dma((R,)), dma((3,)), dma((R,)),
        ],
        compiler_params=pltpu.CompilerParams(vmem_limit_bytes=60 * 2**20),
        name="lag_product",
    )(stack, table)


def shards(spectra, window_flags, source_block, offset_limit):
    rows, cols, table = (jnp.asarray(v, jnp.bfloat16) for v in constants())
    spec = spectra.reshape(2, 256, F)
    stack = fused(source_block, offset_limit, window_flags, spec, rows, cols)
    out = lags(stack, table)
    return out.reshape(R, 8, 32, 2 * F)


def solution(mesh):
    in_specs = (P(None, "chan", "win", None), P("win"), P(), P())
    out_specs = P(None, "win", "chan", None)
    return jax.shard_map(shards, mesh=mesh, in_specs=in_specs, out_specs=out_specs, check_vma=False)
```

```python
import math

import jax
import jax.numpy as jnp
import numpy as np
from jax import lax
from jax.experimental import pallas as pl
from jax.experimental.pallas import tpu as pltpu
from jax.sharding import PartitionSpec as P

MESH = pl.DeviceIdType.MESH
F = 768
HALF = 384
R = 4
SCALE = 1.0 / math.sqrt(24576.0)


def constants():
    rows = np.zeros((256, 256), np.float32)
    for wp in range(4):
        for p in range(4):
            for w2 in range(2):
                for c in range(8):
                    rows[((wp * 4 + p) * 2 + w2) * 8 + c, (p * 8 + c) * 8 + wp * 2 + w2] = 1.0
    cols = np.zeros((256, 256), np.float32)
    for i in range(128):
        cols[2 * i, i] = 1.0
        cols[2 * i + 1, 128 + i] = 1.0
    k = (256 * np.arange(3)[:, None] + 2 * np.arange(128)[None, :]).reshape(-1)
    lag = np.arange(768) - 768
    table = np.zeros((2, 768, 768), np.float32)
    for h in range(2):
        kk = k + h
        m = (kk[:, None] * lag[None, :]) % 1536
        g = np.where(kk == 0, 1.0, 2.0)[:, None]
        table[h, :HALF] = g * np.cos(np.pi * m / 768.0)
        table[h, HALF:] = -g * np.sin(np.pi * m / 768.0)
    return rows, cols, table


def coords():
    c, w = lax.axis_index("chan"), lax.axis_index("win")
    return c // 8, (c // 2) % 4, c % 2, w


def dev(x, z, yh, j):
    return (x * 8 + z * 2 + yh, j)


def whiten_into(spec_ref, flag_ref, rows_ref, cols_ref, out):
    whole = []
    for reim in range(2):
        moved = jnp.dot(rows_ref[...], spec_ref[reim], preferred_element_type=jnp.float32).astype(jnp.bfloat16)
        cut = [
            jnp.dot(moved[:, 256 * b:256 * b + 256], cols_ref[...], preferred_element_type=jnp.float32)
            for b in range(3)
        ]
        whole.append([jnp.concatenate([c[:, 128 * h:128 * h + 128] for c in cut], axis=1) for h in range(2)])
    for wp in range(4):
        part = [[v[64 * wp:64 * wp + 64] for v in pair] for pair in whole]
        (re0, re1), (im0, im1) = part
        p0 = re0 * re0 + im0 * im0
        p1 = re1 * re1 + im1 * im1
        level = (jnp.sum(p0, axis=1, keepdims=True) + jnp.sum(p1, axis=1, keepdims=True)) * (1.0 / F)
        base = 0.25 * level + 1e-06
        row = lax.broadcasted_iota(jnp.int32, (64, 1), 0)
        f0 = flag_ref[2 * wp].astype(jnp.float32)
        f1 = flag_ref[2 * wp + 1].astype(jnp.float32)
        flag = jnp.where((row // 8) % 2 == 0, f0, f1)
        q0 = lax.rsqrt(p0 + base) * flag
        q1 = lax.rsqrt(p1 + base) * flag
        for reim, h, v in ((0, 0, re0 * q0), (0, 1, re1 * q1), (1, 0, im0 * q0), (1, 1, im1 * q1)):
            v = v.astype(jnp.bfloat16).reshape(4, 16, HALF)
            for b in range(3):
                out[b, reim * 8 + wp * 2 + h] = v[:, :, 128 * b:128 * b + 128]


def spread_receivers(recv, b, xr, xi, xs):
    @pl.loop(0, 4)
    def _(a):
        for wp in range(4):
            n = a * 4 + wp
            for h in range(2):
                for p in range(4):
                    re = recv[a, b, wp * 2 + h, p].astype(jnp.float32)
                    im = recv[a, b, 8 + wp * 2 + h, p].astype(jnp.float32)
                    for w2 in range(2):
                        cut = slice(8 * w2, 8 * w2 + 8)
                        xr[h, n * 2 + w2, p] = re[cut]
                        xi[h, n * 2 + w2, p] = im[cut]
                        xs[h, n * 2 + w2, p] = re[cut] + im[cut]


def spread_sources(src, b, r, yr, yi, yd):
    for n in range(16):
        a, wp = n // 4, n % 4
        for h in range(2):
            lo, hi = wp * 2 + h, 8 + wp * 2 + h
            vr = src[b, a // 2, r, lo // 4, lo % 4, a % 2].astype(jnp.float32)
            vi = src[b, a // 2, r, hi // 4, hi % 4, a % 2].astype(jnp.float32)
            for w2 in range(2):
                cr = vr[8 * w2:8 * w2 + 8]
                ci = vi[8 * w2:8 * w2 + 8]
                yr[h, n * 2 + w2] = cr
                yi[h, n * 2 + w2] = ci
                yd[h, n * 2 + w2] = cr - ci


VMEM = 56 * 2**20
SB = 4
UNROLL = 32


def cross_round(xr, xi, xs, yr, yi, yd, stack, r, b, root, limit, chan, member):
    c8 = lax.broadcasted_iota(jnp.int32, (8, 1), 0)

    @pl.loop(0, 2)
    def _(h):
        for s0 in range(0, 8, SB):
            def step(w, acc):
                acc = list(acc)
                for u in range(UNROLL):
                    ww = w * UNROLL + u
                    ar = [xr[h, ww, p] for p in range(4)]
                    ai = [xi[h, ww, p] for p in range(4)]
                    asum = [xs[h, ww, p] for p in range(4)]
                    for s in range(SB):
                        br = jnp.broadcast_to(yr[h, ww, pl.ds(s0 + s, 1)], (8, 128))
                        bi = jnp.broadcast_to(yi[h, ww, pl.ds(s0 + s, 1)], (8, 128))
                        bd = jnp.broadcast_to(yd[h, ww, pl.ds(s0 + s, 1)], (8, 128))
                        for p in range(4):
                            i = (s * 4 + p) * 3
                            acc[i] = acc[i] + ar[p] * br
                            acc[i + 1] = acc[i + 1] + ai[p] * bi
                            acc[i + 2] = acc[i + 2] + asum[p] * bd
                return tuple(acc)

            zero = jnp.zeros((8, 128), jnp.float32)
            acc = lax.fori_loop(0, 32 // UNROLL, step, (zero,) * (SB * 12))
            for s in range(SB):
                sender = root * 32 + member * 8 + s0 + s
                re, im = [], []
                for p in range(4):
                    p1, p2, p3 = acc[(s * 4 + p) * 3:(s * 4 + p) * 3 + 3]
                    gap = jnp.abs(chan * 32 + p * 8 + c8 - sender)
                    keep = jnp.where((gap >= 1) & (gap <= limit), SCALE, 0.0)
                    re.append((p1 + p2) * keep)
                    im.append((p3 - p1 + p2) * keep)
                row = (s0 + s) * 32
                stack[b, r, h, 0, pl.ds(row, 32), :] = jnp.concatenate(re, axis=0).astype(jnp.bfloat16)
                stack[b, r, h, 1, pl.ds(row, 32), :] = jnp.concatenate(im, axis=0).astype(jnp.bfloat16)


def kernel(block_ref, limit_ref, flag_ref, spec_hbm, rows_hbm, cols_hbm, out_hbm,
           spec, rows, cols, recv, cand0, cand1, cand2, pick, diag0, diag1, diag2, src, xr, xi, xs, yr, yi, yd, stack,
           a_s, a_r, d_s, d_r, p_s, p_r, g_s, g_r, f_s, f_r, i_s, o_s, t_s, t_r, u_s, u_r):
    x, z, yh, j = coords()
    slot = x * 4 + z
    cand, diag = (cand0, cand1, cand2), (diag0, diag1, diag2)
    bar = pltpu.get_barrier_semaphore()
    plane = []
    for t in range(1, 16):
        to = (slot + t) % 16
        plane.append((to, dev(to // 4, to % 4, yh, j)))
    column = []
    for t in range(1, 8):
        column.append((t, (j + t) % 4, dev(x, z, (yh + t // 4) % 2, (j + t) % 4)))
    loads = [
        pltpu.make_async_copy(s, d, i_s.at[n])
        for n, (s, d) in enumerate(((spec_hbm, spec), (rows_hbm, rows), (cols_hbm, cols)))
    ]
    for c in loads:
        c.start()
    for _, d in plane:
        pl.semaphore_signal(bar, inc=1, device_id=d, device_id_type=MESH)
    for _, _, d in column:
        pl.semaphore_signal(bar, inc=1, device_id=d, device_id_type=MESH)

    for c in loads:
        c.wait()
    whiten_into(spec, flag_ref, rows, cols, recv.at[j])
    pl.semaphore_wait(bar, 22)
    sends = []

    def remote(s, d, ss, rs, to):
        return pltpu.make_async_remote_copy(
            src_ref=s, dst_ref=d, send_sem=ss, recv_sem=rs, device_id=to, device_id_type=MESH)

    def send(*args):
        c = remote(*args)
        c.start()
        sends.append(c)
        return c

    mate = dev(x, z, yh, j + 1 - 2 * (j % 2))
    across = (j + 2) % 4
    other = dev(x, z, yh, across)
    swap = []

    def exchange(b):
        swap.append([
            send(recv.at[j, b, to], cand[b].at[slot], a_s.at[b, t], a_r.at[b, t], d)
            for t, (to, d) in enumerate(plane)
        ])

    exchange(0)
    over = []

    def cross_over(b):
        over.append(send(recv.at[j, b], recv.at[j, b], g_s.at[b], g_r.at[b], other))

    cross_over(0)
    to_mate = [send(recv.at[j, b], recv.at[j, b], p_s.at[b], p_r.at[b], mate) for b in range(3)]
    for b in range(3):
        cand[b][slot] = recv[j, b, slot]

    def relay(b):
        over[b].wait_recv()
        return send(recv.at[across, b], recv.at[across, b], f_s.at[b], f_r.at[b], mate)

    def choose(b):
        for c in swap[b]:
            c.wait_recv()
        for r in range(R):
            pick[b, :, r] = cand[b][block_ref[r] // 2]
        diag[b][yh, j] = pick[b, j]
        return [send(pick.at[b, p], diag[b].at[yh, j], d_s.at[b, t], d_r.at[b, t], d) for t, p, d in column]

    def gather(b, meet):
        for c in meet:
            c.wait_recv()
        for r in range(R):
            got = diag[b][block_ref[r] % 2, :, r]
            src[b, 0, r, x, z] = got[0:2]
            src[b, 1, r, x, z] = got[2:4]
        out = []
        for d in range(1, 4):
            z2, x2 = (z + d) % 4, (x + d) % 4
            out.append(send(src.at[b, 0, :, x, z], src.at[b, 0, :, x, z], t_s.at[b, 0, d], t_r.at[b, 0, d], dev(x, z2, yh, j)))
            out.append(send(src.at[b, 1, :, x, z], src.at[b, 1, :, x, z], t_s.at[b, 1, d], t_r.at[b, 1, d], dev(x2, z, yh, j)))
        return out

    def spread(b, r, d):
        z2, x2 = (z + d) % 4, (x + d) % 4
        return (
            remote(src.at[b, 0, r, x], src.at[b, 0, r, x], u_s.at[b, 0, r, d], u_r.at[b, 0, r, d], dev(x2, z, yh, j)),
            remote(src.at[b, 1, r, :, z], src.at[b, 1, r, :, z], u_s.at[b, 1, r, d], u_r.at[b, 1, r, d], dev(x, z2, yh, j)),
        )

    def scatter(b, first, rounds):
        for c in first:
            c.wait_recv()
        for r in rounds:
            for d in range(1, 4):
                for c in spread(b, r, d):
                    c.start()

    chan = x * 8 + z * 2 + yh
    relayed = []

    def receivers(b):
        to_mate[b].wait_recv()
        relayed[b].wait_recv()
        spread_receivers(recv, b, xr, xi, xs)

    def arrived(b, r):
        for d in range(1, 4):
            for c in spread(b, r, d):
                c.wait_recv()

    def compute(b, r):
        spread_sources(src, b, r, yr, yi, yd)
        cross_round(xr, xi, xs, yr, yi, yd, stack, r, b, block_ref[r], limit_ref[r], chan, j)
        pltpu.make_async_copy(stack.at[b, r], out_hbm.at[b, r], o_s.at[b, r]).start()

    swap[0].pop(0).wait_recv()
    exchange(1)
    m0 = choose(0)
    exchange(2)
    m1 = choose(1)
    f0 = gather(0, m0)
    cross_over(1)
    relayed.append(relay(0))
    m2 = choose(2)
    scatter(0, f0, range(R))
    f1 = gather(1, m1)
    f2 = gather(2, m2)
    cross_over(2)
    receivers(0)
    arrived(0, 0)
    compute(0, 0)
    scatter(1, f1, range(R))
    arrived(0, 1)
    compute(0, 1)
    scatter(2, f2, range(R))
    relayed.append(relay(1))

    @pl.loop(2, R)
    def _(r):
        arrived(0, r)
        compute(0, r)

    relayed.append(relay(2))
    for b in (1, 2):
        receivers(b)

        @pl.loop(0, R)
        def _(r):
            arrived(b, r)
            compute(b, r)

    for r in range(R):
        for b in range(3):
            pltpu.make_async_copy(stack.at[b, r], out_hbm.at[b, r], o_s.at[b, r]).wait()
            for d in range(1, 4):
                for c in spread(b, r, d):
                    c.wait_send()
    for c in sends:
        c.wait_send()


def fused(block, limit, flags, spec, rows, cols):
    bf, f32 = jnp.bfloat16, jnp.float32
    dma = pltpu.SemaphoreType.DMA
    hbm = pl.BlockSpec(memory_space=pl.ANY)
    sm = pl.BlockSpec(memory_space=pltpu.SMEM)
    vm = pltpu.VMEM
    return pl.pallas_call(
        kernel,
        out_shape=jax.ShapeDtypeStruct((3, R, 2, 2, 256, 128), bf),
        in_specs=[sm, sm, sm, hbm, hbm, hbm],
        out_specs=hbm,
        scratch_shapes=[
            vm((2, 256, F), bf), vm((256, 256), bf), vm((256, 256), bf),
            vm((4, 3, 16, 4, 16, 128), bf),
            vm((16, 4, 16, 128), bf), vm((16, 4, 16, 128), bf), vm((16, 4, 16, 128), bf),
            vm((3, 4, R, 16, 128), bf),
            vm((2, 4, R, 16, 128), bf), vm((2, 4, R, 16, 128), bf), vm((2, 4, R, 16, 128), bf),
            vm((3, 2, R, 4, 4, 2, 16, 128), bf),
            vm((2, 32, 4, 8, 128), f32), vm((2, 32, 4, 8, 128), f32), vm((2, 32, 4, 8, 128), f32),
            vm((2, 32, 8, 128), f32), vm((2, 32, 8, 128), f32), vm((2, 32, 8, 128), f32),
            vm((3, R, 2, 2, 256, 128), bf),
            dma((3, 16)), dma((3, 16)), dma((3, 8)), dma((3, 8)), dma((3,)), dma((3,)),
            dma((3,)), dma((3,)), dma((3,)), dma((3,)), dma((3,)), dma((3, R)),
            dma((3, 2, 4)), dma((3, 2, 4)), dma((3, 2, R, 4)), dma((3, 2, R, 4)),
        ],
        compiler_params=pltpu.CompilerParams(
            collective_id=1, has_side_effects=True, vmem_limit_bytes=VMEM),
        name="whiten_correlate",
    )(block, limit, flags, spec, rows, cols)


def lag_kernel(stack_hbm, table_hbm, out_hbm, stack, table, out, s_sem, t_sem, o_sem):
    takes = [pltpu.make_async_copy(stack_hbm.at[:, r], stack.at[r], s_sem.at[r]) for r in range(R)]
    cols = [
        pltpu.make_async_copy(table_hbm.at[:, :, pl.ds(256 * n, 256)], table.at[n], t_sem.at[n]) for n in range(3)
    ]
    takes[0].start()
    for c in cols:
        c.start()
    for c in takes[1:]:
        c.start()
    puts = []
    for r in range(R):
        takes[r].wait()
        lhs = [jnp.concatenate([stack[r, b, h, q] for q in range(2) for b in range(3)], axis=1) for h in range(2)]
        for n in range(3):
            if r == 0:
                cols[n].wait()
            e = jnp.dot(lhs[0], table[n, 0], preferred_element_type=jnp.float32)
            o = jnp.dot(lhs[1], table[n, 1], preferred_element_type=jnp.float32)
            out[r, :, pl.ds(256 * n, 256)] = (e + o).astype(jnp.bfloat16)
            out[r, :, pl.ds(768 + 256 * n, 256)] = (e - o).astype(jnp.bfloat16)
        puts.append(pltpu.make_async_copy(out.at[r], out_hbm.at[r], o_sem.at[r]))
        puts[-1].start()
    for c in puts:
        c.wait()


def lags(stack, table):
    bf, dma = jnp.bfloat16, pltpu.SemaphoreType.DMA
    hbm = pl.BlockSpec(memory_space=pl.ANY)
    return pl.pallas_call(
        lag_kernel,
        out_shape=jax.ShapeDtypeStruct((R, 256, 2 * F), bf),
        in_specs=[hbm, hbm],
        out_specs=hbm,
        scratch_shapes=[
            pltpu.VMEM((R, 3, 2, 2, 256, 128), bf),
            pltpu.VMEM((3, 2, F, 256), bf),
            pltpu.VMEM((R, 256, 2 * F), bf),
            dma((R,)), dma((3,)), dma((R,)),
        ],
        compiler_params=pltpu.CompilerParams(vmem_limit_bytes=60 * 2**20),
        name="lag_product",
    )(stack, table)


def shards(spectra, window_flags, source_block, offset_limit):
    rows, cols, table = (jnp.asarray(v, jnp.bfloat16) for v in constants())
    spec = spectra.reshape(2, 256, F)
    stack = fused(source_block, offset_limit, window_flags, spec, rows, cols)
    out = lags(stack, table)
    return out.reshape(R, 8, 32, 2 * F)


def solution(mesh):
    in_specs = (P(None, "chan", "win", None), P("win"), P(), P())
    out_specs = P(None, "win", "chan", None)
    return jax.shard_map(shards, mesh=mesh, in_specs=in_specs, out_specs=out_specs, check_vma=False)
```
